32 devices in a mesh: mem: 2 (over x), par: 16 (over z, y, core).
Axes of the slice: x: 2, y: 2, z: 4, core: 2. Of those that a mesh axis runs over, the one named last changes fastest.
Arguments:
- operator: float32 [32768, 512], P('par'), may hold values from -0.046875 to 0.046875
- ensemble: float32 [256, 32768], P('mem', 'par'), may hold values from -6 to 6
- noise: float32 [256, 512], P('mem'), may hold values from -6 to 6
- observations: float32 [16384], replicated, may hold values from -6 to 6
- variances: float32 [16384], replicated, may hold values from 0.25 to 4
- rows: int32 [512], replicated, may hold values from 0 to 16383
Outputs:
- updated: float32 [256, 32768], P('mem', 'par')
The draws below stay inside these ranges and needn't reach their ends.
Inputs may be any that keep to these rules, and one draw needn't show every extreme that they name: `rows`: indices into the observations; they may repeat.
All inputs are finite; a program needn't handle non-finite values.
Results may differ from the reference program's by a relative error of at most 0.00017.
Values sent between devices are 32-bit elements; how exact they have to be, the bound alone decides.
No kernel may reach another device: no remote copies, remote signals or barrier semaphores. Data moves between devices by JAX's collectives and lax.ppermute only.
A program may use at most 64 MiB of HBM per device.

```python
import math
import jax
import jax.numpy as jnp
from jax import lax

MEMBERS = 256
ROWS = 512
OBS = 16384
PARAMS = 32768


def touch_ends(result, stream_key, low, high):
    spot = [jax.random.randint(jax.random.fold_in(stream_key, axis), (), 0, length) for axis, length in enumerate(result.shape)]
    widest = result.shape.index(max(result.shape))
    neighbour = spot[:widest] + [(spot[widest] + 1) % result.shape[widest]] + spot[widest + 1:]
    return result.at[tuple(spot)].set(low).at[tuple(neighbour)].set(high)


def spiked(result, rng, source, target, parts, factor):
    def block_of(position):
        return (jnp.arange(result.shape[position]) // (result.shape[position] // parts)).reshape((-1,) + (1,) * (result.ndim - 1 - position))

    near = jax.random.permutation(rng, parts)[block_of(target)]
    other_side = (block_of(target) + parts // 2) % parts
    return jnp.where((block_of(source) == near) | (block_of(source) == other_side), factor * result, result)


def block_levels(key, shape, split, smallest, top_value):
    def one(axis_at, shards_of):
        draws = jax.random.uniform(jax.random.fold_in(jax.random.fold_in(key, 6), axis_at), (shards_of,), jnp.float32, smallest / len(split), top_value / len(split))
        return jnp.repeat(jnp.exp(draws), shape[axis_at] // shards_of).reshape((-1,) + (1,) * (len(shape) - axis_at - 1))

    factor_of = one(*split[0])
    for cut in split[1:]:
        factor_of = factor_of * one(*cut)
    return factor_of


def normal_values(rng, dims, scale, bound, cuts=(), kind=jnp.bfloat16):
    entries = scale * jax.random.normal(rng, dims, jnp.float32)
    if cuts:
        entries = entries * block_levels(rng, dims, cuts, -0.22, 0.18)
    return jnp.clip(entries, -bound, bound).astype(kind)


def heavy_noise(key, extent, scale, reach, pieces, heavy, held_as=jnp.bfloat16):
    values = scale * jax.random.normal(key, extent, jnp.float32)
    if pieces:
        values = values * block_levels(key, extent, pieces, -0.22, 0.18)
    return jnp.clip(spiked(values, jax.random.fold_in(key, 3), *heavy), -reach, reach).astype(held_as)


def setup_inputs(seed: int = 0) -> dict:
    keys = jax.random.split(jax.random.key(seed), 7)
    return {
        "operator": heavy_noise(keys[0], (PARAMS, ROWS), PARAMS ** -0.5, 0.046875, ((0, 16),), (0, 1, 16, 2.0), jnp.float32),
        "ensemble": normal_values(keys[1], (MEMBERS, PARAMS), 1.0, 6.0, ((0, 2), (1, 16)), jnp.float32),
        "noise": normal_values(keys[2], (MEMBERS, ROWS), 1.0, 6.0, ((0, 2),), jnp.float32),
        "observations": normal_values(keys[3], (OBS,), 1.0, 6.0, (), jnp.float32),
        "variances": jnp.clip(jnp.exp(jax.random.uniform(keys[4], (OBS,), jnp.float32, math.log(0.25), math.log(4.0))), 0.25, 4.0),
        "rows": touch_ends(jax.random.randint(keys[5], (ROWS,), 0, OBS), jax.random.fold_in(keys[5], 1), 0, OBS - 1).astype(jnp.int32),
    }


def cholesky_solve(matrix, right):
    factor = jnp.linalg.cholesky(matrix)
    inner = lax.linalg.triangular_solve(factor, right, left_side=True, lower=True)
    return lax.linalg.triangular_solve(factor, inner, left_side=True, lower=True, transpose_a=True)

def reference(operator, ensemble, noise, observations, variances, rows):
    highest = lax.Precision.HIGHEST
    forward = jnp.dot(ensemble.astype(jnp.float32), operator.astype(jnp.float32), precision=highest, preferred_element_type=jnp.float32)
    obs_rows = jnp.take(observations, rows)
    var_rows = jnp.take(variances, rows)
    residual = obs_rows[None, :] + jnp.sqrt(var_rows)[None, :] * noise - forward
    spread = forward - lax.optimization_barrier(jnp.mean(forward, axis=0, keepdims=True))
    weighted = spread / var_rows[None, :]
    count = forward.shape[0]
    gram = jnp.dot(weighted.astype(jnp.float32), spread.T.astype(jnp.float32), precision=highest, preferred_element_type=jnp.float32)
    gram = gram + (count - 1) * jnp.eye(count, dtype=jnp.float32)
    cross = jnp.dot(weighted.astype(jnp.float32), residual.T.astype(jnp.float32), precision=highest, preferred_element_type=jnp.float32)
    weights = cholesky_solve(gram, cross)
    deviation = ensemble - lax.optimization_barrier(jnp.mean(ensemble, axis=0, keepdims=True))
    return ensemble + jnp.dot(weights.T.astype(jnp.float32), deviation.astype(jnp.float32), precision=highest, preferred_element_type=jnp.float32)
```

```python
import functools

import jax
import jax.numpy as jnp
from jax import lax
from jax.experimental import pallas as pl
from jax.experimental.pallas import tpu as pltpu
from jax.sharding import PartitionSpec as P

f32 = jnp.float32
HIGHEST = lax.Precision.HIGHEST
SUB, LANE = 8, 128
VMEM = pl.BlockSpec(memory_space=pltpu.VMEM)
SMEM = pl.BlockSpec(memory_space=pltpu.SMEM)
ANY = pl.BlockSpec(memory_space=pl.ANY)


def dot(a, b, dims, precision=HIGHEST):
    return lax.dot_general(a, b, (dims, ((), ())), precision=precision, preferred_element_type=f32)


def add_all(terms):
    terms = list(terms)
    while len(terms) > 1:
        pairs = [terms[i] + terms[i + 1] for i in range(0, len(terms) - 1, 2)]
        terms = pairs + ([terms[-1]] if len(terms) % 2 else [])
    return terms[0]


def small_inverse(e):
    n = len(e)

    def at(m, i, k):
        return m[min(i, k)][max(i, k)]

    if n == 2:
        a, b, c = e[0][0], e[0][1], e[1][1]
        d = 1.0 / (a * c - b * b)
        return [[c * d, -(b * d)], [None, a * d]]
    m = n // 2
    span = range(m)
    top = small_inverse([[at(e, i, k) for k in span] for i in span])
    side = [[at(e, i, m + k) for k in span] for i in span]
    t = [[add_all(at(top, i, l) * side[l][k] for l in span) for k in span] for i in span]
    rest = [
        [at(e, m + i, m + k) - add_all(side[l][i] * t[l][k] for l in span) if i <= k else None for k in span]
        for i in span
    ]
    low = small_inverse(rest)
    u = [[add_all(t[i][l] * at(low, l, k) for l in span) for k in span] for i in span]
    out = [[None] * n for _ in range(n)]
    for i in span:
        for k in span:
            if i <= k:
                out[i][k] = top[i][k] + add_all(u[i][l] * t[k][l] for l in span)
                out[m + i][m + k] = low[i][k]
            out[i][m + k] = -u[i][k]
    return out


def across(v, k):
    return jnp.broadcast_to(v[:, k : k + 1], v.shape)


def down(v, i):
    return jnp.broadcast_to(v[i : i + 1, :], v.shape)


def block_inverse(matrix):
    lane = lax.broadcasted_iota(jnp.int32, (SUB, LANE), 1)
    sub = lax.broadcasted_iota(jnp.int32, (SUB, LANE), 0)
    n = LANE // SUB
    m = [matrix[SUB * i : SUB * (i + 1), :] for i in range(n)]
    for j in range(n):
        at = SUB * j
        here = (lane >= at) & (lane < at + SUB)
        cols = [across(m[j], at + k) for k in range(SUB)]
        inv = small_inverse([[down(cols[k], i) if i <= k else None for k in range(SUB)] for i in range(SUB)])
        row = jnp.where(here, (lane - at == sub).astype(f32), m[j])
        rows = [down(row, k) for k in range(SUB)]
        new = [add_all(inv[min(i, k)][max(i, k)] * rows[k] for k in range(SUB)) for i in range(SUB)]
        for d in range(1, n):
            i = (j + d) % n
            drop = add_all(across(m[i], at + k) * new[k] for k in range(SUB))
            m[i] = jnp.where(here, 0.0, m[i]) - drop
        done = new[0]
        for i in range(1, SUB):
            done = jnp.where(sub == i, new[i], done)
        m[j] = done
    return jnp.concatenate(m, axis=0)


def forward_kernel(bits, ens, op, keep, send, acc):
    step = pl.program_id(0)

    @pl.when(step == 0)
    def _():
        acc[...] = jnp.zeros_like(acc)

    acc[...] += dot(ens[...], op[...], ((1,), (0,)))

    @pl.when(step == pl.num_programs(0) - 1)
    def _():
        half = keep.shape[0]
        mine = pl.multiple_of(bits[0] * half, SUB)
        other = pl.multiple_of((1 - bits[0]) * half, SUB)
        keep[...] = acc[pl.ds(mine, half), :]
        send[...] = acc[pl.ds(other, half), :]


def forward(ens, op, bits):
    members, params = ens.shape
    rows = op.shape[1]
    steps = 4 if params % (4 * LANE) == 0 else 1
    depth = params // steps
    half = jax.ShapeDtypeStruct((members // 2, rows), f32)
    whole = pl.BlockSpec((members // 2, rows), lambda i: (0, 0))
    return pl.pallas_call(
        forward_kernel,
        grid=(steps,),
        out_shape=(half, half),
        in_specs=[
            SMEM,
            pl.BlockSpec((members, depth), lambda i: (0, i)),
            pl.BlockSpec((depth, rows), lambda i: (i, 0)),
        ],
        out_specs=(whole, whole),
        scratch_shapes=[pltpu.VMEM((members, rows), f32)],
        cost_estimate=pl.CostEstimate(
            flops=2 * members * params * rows, bytes_accessed=4 * (members * params + params * rows), transcendentals=0
        ),
        name="forward",
    )(bits, ens, op)


def lookup_kernel(rows, obs, var, noise, target, inverse_var):
    index = rows[...]
    high = lax.shift_right_logical(index, 7)
    low = lax.bitwise_and(index, LANE - 1)
    count = index.shape[1]
    blocks = obs.shape[0]
    pick_high = (lax.broadcasted_iota(jnp.int32, (blocks, count), 0) == high).astype(f32)
    pick_low = (lax.broadcasted_iota(jnp.int32, (LANE, count), 0) == low).astype(f32)
    obs_rows = jnp.sum(dot(obs[...], pick_high, ((0,), (0,))) * pick_low, axis=0, keepdims=True)
    var_rows = jnp.sum(dot(var[...], pick_high, ((0,), (0,))) * pick_low, axis=0, keepdims=True)
    target[...] = obs_rows + jnp.sqrt(var_rows) * noise[...]
    inverse_var[...] = jnp.broadcast_to(1.0 / var_rows, inverse_var.shape)


def lookup(rows, obs, var, noise):
    count = rows.shape[0]
    return pl.pallas_call(
        lookup_kernel,
        out_shape=(
            jax.ShapeDtypeStruct(noise.shape, f32),
            jax.ShapeDtypeStruct((SUB, count), f32),
        ),
        in_specs=[VMEM] * 4,
        out_specs=(VMEM, VMEM),
        cost_estimate=pl.CostEstimate(flops=2 * obs.shape[0] * LANE * count * 12, bytes_accessed=1 << 20, transcendentals=0),
        name="lookup",
    )(rows.reshape(1, count), obs.reshape(-1, LANE), var.reshape(-1, LANE), noise)


def solve_kernel(places, own, bits, *refs):
    count = len(places)
    pieces = refs[:count]
    target, inverse_var = refs[count : count + 2]
    weights = refs[count + 2]
    fwd = refs[count + 3]
    rows = pieces[0].shape[0]
    for piece, (far, dy, dc) in zip(pieces, places):
        core = bits[0] if dc == 0 else 1 - bits[0]
        side = bits[1] if dy == 0 else 1 - bits[1]
        fwd[pl.ds(pl.multiple_of(far * own + (core * 2 + side) * rows, SUB), rows), :] = piece[...]
    members = fwd.shape[0]
    spread = fwd[...] - jnp.mean(fwd[...], axis=0, keepdims=True)
    weighted = spread * inverse_var[0:1, :]
    gram = dot(weighted, spread, ((1,), (1,)))
    cross = dot(weighted, target[...] - fwd[0:own, :], ((1,), (1,)))
    blocks = members // LANE
    eye = (
        lax.broadcasted_iota(jnp.int32, (LANE, LANE), 0) == lax.broadcasted_iota(jnp.int32, (LANE, LANE), 1)
    ).astype(f32) * (members - 1)
    cut = lambda i: slice(i * LANE, (i + 1) * LANE)
    g = [[gram[cut(i), cut(k)] + (eye if i == k else 0.0) for k in range(blocks)] for i in range(blocks)]
    c = [cross[cut(i), :] for i in range(blocks)]
    t = [[None] * blocks for _ in range(blocks)]
    for j in range(blocks):
        inv = block_inverse(g[j][j])
        c[j] = dot(inv, c[j], ((1,), (0,)))
        for k in range(j + 1, blocks):
            t[j][k] = dot(inv, g[j][k], ((1,), (0,)))
        for i in range(j + 1, blocks):
            c[i] = c[i] - dot(g[i][j], c[j], ((1,), (0,)))
            for k in range(j + 1, blocks):
                g[i][k] = g[i][k] - dot(g[i][j], t[j][k], ((1,), (0,)))
    for j in reversed(range(blocks)):
        for k in range(j + 1, blocks):
            c[j] = c[j] - dot(t[j][k], c[k], ((1,), (0,)))
    w = jnp.concatenate(c, axis=0)
    weights[...] = (w - jnp.mean(w, axis=0, keepdims=True)).T


def solve(pieces, places, target, inverse_var, bits, members):
    own, rows = target.shape
    return pl.pallas_call(
        functools.partial(solve_kernel, places, own),
        out_shape=jax.ShapeDtypeStruct((own, members), f32),
        in_specs=[SMEM] + [VMEM] * (len(pieces) + 2),
        out_specs=VMEM,
        scratch_shapes=[pltpu.VMEM((members, rows), f32)],
        cost_estimate=pl.CostEstimate(flops=2 * members * members * rows * 12, bytes_accessed=1 << 20, transcendentals=0),
        name="solve",
    )(bits, *pieces, target, inverse_var)


def update_kernel(weights, *refs):
    out = refs[-1]
    ens = refs[:-1]
    own = ens[0].shape[0]
    total = ens[0][...]
    for far, part in enumerate(ens):
        total = total + dot(weights[:, far * own : (far + 1) * own], part[...], ((1,), (0,)))
    out[...] = total


def update(weights, ens):
    own, params = ens[0].shape
    steps = 4 if params % (4 * LANE) == 0 else 1
    block = pl.BlockSpec((own, params // steps), lambda i: (0, i))
    return pl.pallas_call(
        update_kernel,
        grid=(steps,),
        out_shape=jax.ShapeDtypeStruct((own, params), f32),
        in_specs=[pl.BlockSpec(weights.shape, lambda i: (0, 0))] + [block] * len(ens),
        out_specs=block,
        cost_estimate=pl.CostEstimate(
            flops=2 * own * weights.shape[1] * params, bytes_accessed=4 * params * (own + weights.shape[1]), transcendentals=0
        ),
        name="update",
    )(weights, *ens)


def per_device(n_mem, n_par, operator, ensemble, noise, observations, variances, rows):
    index = lax.axis_index("par")
    core, side = index % 2, (index // 2) % 2
    bits = jnp.stack([core, side]).astype(jnp.int32)

    def swap(x, far, near):
        pairs = [
            (m * n_par + p, (m ^ far) * n_par + (p ^ near)) for m in range(n_mem) for p in range(n_par)
        ]
        return lax.ppermute(x, ("mem", "par"), pairs)

    ens = [ensemble] + [swap(ensemble, far, 0) for far in range(1, n_mem)]
    keep, send = forward(ensemble, operator, bits)
    part = keep + swap(send, 0, 1)
    size = part.shape[0] // 2
    total = lax.dynamic_slice_in_dim(part, side * size, size, 0) + swap(
        lax.dynamic_slice_in_dim(part, (1 - side) * size, size, 0), 0, 2
    )
    stride = 4
    while stride < n_par:
        ways = min(4, n_par // stride)
        total = add_all([total] + [swap(total, 0, d * stride) for d in range(1, ways)])
        stride *= ways
    target, inverse_var = lookup(rows, observations, variances, noise)
    places = [(far, dy, 0) for far in range(n_mem) for dy in range(2)]
    pieces = [total if (far, dy) == (0, 0) else swap(total, far, 2 * dy) for far, dy, _ in places]
    pieces += [swap(piece, 0, 1) for piece in pieces]
    places += [(far, dy, 1) for far, dy, _ in places]
    members = ensemble.shape[0] * n_mem
    weights = solve(pieces, places, target, inverse_var, bits, members)
    return update(weights, ens)


def solution(mesh):
    return jax.shard_map(
        functools.partial(per_device, mesh.shape["mem"], mesh.shape["par"]),
        mesh=mesh,
        in_specs=(P("par", None), P("mem", "par"), P("mem", None), P(), P(), P()),
        out_specs=P("mem", "par"),
        check_vma=False,
    )
```

```python
import functools

import jax
import jax.numpy as jnp
from jax import lax
from jax.experimental import pallas as pl
from jax.experimental.pallas import tpu as pltpu
from jax.sharding import PartitionSpec as P

f32 = jnp.float32
HIGHEST = lax.Precision.HIGHEST
SUB, LANE = 8, 128
VMEM = pl.BlockSpec(memory_space=pltpu.VMEM)
VMEM_LIMIT = 20 << 20


def dot(a, b, dims, precision=HIGHEST):
    return lax.dot_general(a, b, (dims, ((), ())), precision=precision, preferred_element_type=f32)


def add_all(terms):
    terms = list(terms)
    while len(terms) > 1:
        pairs = [terms[i] + terms[i + 1] for i in range(0, len(terms) - 1, 2)]
        terms = pairs + ([terms[-1]] if len(terms) % 2 else [])
    return terms[0]


def small_inverse(e):
    n = len(e)

    def at(m, i, k):
        return m[min(i, k)][max(i, k)]

    if n == 2:
        a, b, c = e[0][0], e[0][1], e[1][1]
        d = 1.0 / (a * c - b * b)
        return [[c * d, -(b * d)], [None, a * d]]
    m = n // 2
    span = range(m)
    top = small_inverse([[at(e, i, k) for k in span] for i in span])
    side = [[at(e, i, m + k) for k in span] for i in span]
    t = [[add_all(at(top, i, l) * side[l][k] for l in span) for k in span] for i in span]
    rest = [
        [at(e, m + i, m + k) - add_all(side[l][i] * t[l][k] for l in span) if i <= k else None for k in span]
        for i in span
    ]
    low = small_inverse(rest)
    u = [[add_all(t[i][l] * at(low, l, k) for l in span) for k in span] for i in span]
    out = [[None] * n for _ in range(n)]
    for i in span:
        for k in span:
            if i <= k:
                out[i][k] = top[i][k] + add_all(u[i][l] * t[k][l] for l in span)
                out[m + i][m + k] = low[i][k]
            out[i][m + k] = -u[i][k]
    return out


def across(v, k):
    return jnp.broadcast_to(v[:, k : k + 1], v.shape)


def down(v, i):
    return jnp.broadcast_to(v[i : i + 1, :], v.shape)


def block_inverse(matrix):
    lane = lax.broadcasted_iota(jnp.int32, (SUB, LANE), 1)
    sub = lax.broadcasted_iota(jnp.int32, (SUB, LANE), 0)
    n = LANE // SUB
    m = [matrix[SUB * i : SUB * (i + 1), :] for i in range(n)]
    for j in range(n):
        at = SUB * j
        here = (lane >= at) & (lane < at + SUB)
        cols = [across(m[j], at + k) for k in range(SUB)]
        inv = small_inverse([[down(cols[k], i) if i <= k else None for k in range(SUB)] for i in range(SUB)])
        row = jnp.where(here, (lane - at == sub).astype(f32), m[j])
        rows = [down(row, k) for k in range(SUB)]
        new = [add_all(inv[min(i, k)][max(i, k)] * rows[k] for k in range(SUB)) for i in range(SUB)]
        for d in range(1, n):
            i = (j + d) % n
            drop = add_all(across(m[i], at + k) * new[k] for k in range(SUB))
            m[i] = jnp.where(here, 0.0, m[i]) - drop
        done = new[0]
        for i in range(1, SUB):
            done = jnp.where(sub == i, new[i], done)
        m[j] = done
    return jnp.concatenate(m, axis=0)


def own_bits():
    index = lax.axis_index("par")
    return lax.bitwise_and(index, 1), lax.bitwise_and(lax.shift_right_logical(index, 1), 1)


def forward_kernel(ens, op, keep, send, acc):
    step = pl.program_id(0)

    @pl.when(step == 0)
    def _():
        acc[...] = jnp.zeros_like(acc)

    acc[...] += dot(ens[...], op[...], ((1,), (0,)))

    @pl.when(step == pl.num_programs(0) - 1)
    def _():
        half = keep.shape[0]
        core, _ = own_bits()
        mine = pl.multiple_of(core * half, SUB)
        other = pl.multiple_of((1 - core) * half, SUB)
        keep[...] = acc[pl.ds(mine, half), :]
        send[...] = acc[pl.ds(other, half), :]


def forward(ens, op):
    members, params = ens.shape
    rows = op.shape[1]
    steps = 4 if params % (4 * LANE) == 0 else 1
    depth = params // steps
    half = jax.ShapeDtypeStruct((members // 2, rows), f32)
    whole = pl.BlockSpec((members // 2, rows), lambda i: (0, 0))
    return pl.pallas_call(
        forward_kernel,
        grid=(steps,),
        out_shape=(half, half),
        in_specs=[
            pl.BlockSpec((members, depth), lambda i: (0, i)),
            pl.BlockSpec((depth, rows), lambda i: (i, 0)),
        ],
        out_specs=(whole, whole),
        scratch_shapes=[pltpu.VMEM((members, rows), f32)],
        cost_estimate=pl.CostEstimate(
            flops=2 * members * params * rows, bytes_accessed=4 * (members * params + params * rows), transcendentals=0
        ),
        compiler_params=pltpu.CompilerParams(vmem_limit_bytes=VMEM_LIMIT),
        name="forward",
    )(ens, op)


def lookup_kernel(rows, obs, var, noise, target, inverse_var):
    index = rows[...]
    high = lax.shift_right_logical(index, 7)
    low = lax.bitwise_and(index, LANE - 1)
    count = index.shape[1]
    blocks = obs.shape[0]
    pick_high = (lax.broadcasted_iota(jnp.int32, (blocks, count), 0) == high).astype(f32)
    pick_low = (lax.broadcasted_iota(jnp.int32, (LANE, count), 0) == low).astype(f32)
    obs_rows = jnp.sum(dot(obs[...], pick_high, ((0,), (0,))) * pick_low, axis=0, keepdims=True)
    var_rows = jnp.sum(dot(var[...], pick_high, ((0,), (0,))) * pick_low, axis=0, keepdims=True)
    target[...] = obs_rows + jnp.sqrt(var_rows) * noise[...]
    inverse_var[...] = jnp.broadcast_to(1.0 / var_rows, inverse_var.shape)


def lookup(rows, obs, var, noise):
    count = rows.shape[0]
    return pl.pallas_call(
        lookup_kernel,
        out_shape=(
            jax.ShapeDtypeStruct(noise.shape, f32),
            jax.ShapeDtypeStruct((SUB, count), f32),
        ),
        in_specs=[VMEM] * 4,
        out_specs=(VMEM, VMEM),
        cost_estimate=pl.CostEstimate(flops=2 * obs.shape[0] * LANE * count * 12, bytes_accessed=1 << 20, transcendentals=0),
        compiler_params=pltpu.CompilerParams(vmem_limit_bytes=VMEM_LIMIT),
        name="lookup",
    )(rows.reshape(1, count), obs.reshape(-1, LANE), var.reshape(-1, LANE), noise)


def solve_kernel(places, own, *refs):
    own_core, own_side = own_bits()
    count = len(places)
    pieces = refs[:count]
    target, inverse_var = refs[count : count + 2]
    weights = refs[count + 2]
    fwd = refs[count + 3]
    rows = pieces[0].shape[0]
    for piece, (far, dy, dc) in zip(pieces, places):
        core = own_core if dc == 0 else 1 - own_core
        side = own_side if dy == 0 else 1 - own_side
        fwd[pl.ds(pl.multiple_of(far * own + (core * 2 + side) * rows, SUB), rows), :] = piece[...]
    members = fwd.shape[0]
    spread = fwd[...] - jnp.mean(fwd[...], axis=0, keepdims=True)
    weighted = spread * inverse_var[0:1, :]
    gram = dot(weighted, spread, ((1,), (1,)))
    cross = dot(weighted, target[...] - fwd[0:own, :], ((1,), (1,)))
    blocks = members // LANE
    eye = (
        lax.broadcasted_iota(jnp.int32, (LANE, LANE), 0) == lax.broadcasted_iota(jnp.int32, (LANE, LANE), 1)
    ).astype(f32) * (members - 1)
    cut = lambda i: slice(i * LANE, (i + 1) * LANE)
    g = [[gram[cut(i), cut(k)] + (eye if i == k else 0.0) for k in range(blocks)] for i in range(blocks)]
    c = [cross[cut(i), :] for i in range(blocks)]
    t = [[None] * blocks for _ in range(blocks)]
    for j in range(blocks):
        inv = block_inverse(g[j][j])
        c[j] = dot(inv, c[j], ((1,), (0,)))
        for k in range(j + 1, blocks):
            t[j][k] = dot(inv, g[j][k], ((1,), (0,)))
        for i in range(j + 1, blocks):
            c[i] = c[i] - dot(g[i][j], c[j], ((1,), (0,)))
            for k in range(j + 1, blocks):
                g[i][k] = g[i][k] - dot(g[i][j], t[j][k], ((1,), (0,)))
    for j in reversed(range(blocks)):
        for k in range(j + 1, blocks):
            c[j] = c[j] - dot(t[j][k], c[k], ((1,), (0,)))
    w = jnp.concatenate(c, axis=0)
    weights[...] = (w - jnp.mean(w, axis=0, keepdims=True)).T


def solve(pieces, places, target, inverse_var, members):
    own, rows = target.shape
    return pl.pallas_call(
        functools.partial(solve_kernel, places, own),
        out_shape=jax.ShapeDtypeStruct((own, members), f32),
        in_specs=[VMEM] * (len(pieces) + 2),
        out_specs=VMEM,
        scratch_shapes=[pltpu.VMEM((members, rows), f32)],
        cost_estimate=pl.CostEstimate(flops=1, bytes_accessed=1, transcendentals=0),
        compiler_params=pltpu.CompilerParams(vmem_limit_bytes=VMEM_LIMIT),
        name="solve",
    )(*pieces, target, inverse_var)


def update_kernel(weights, *refs):
    out = refs[-1]
    ens = refs[:-1]
    own = ens[0].shape[0]
    total = ens[0][...]
    for far, part in enumerate(ens):
        total = total + dot(weights[:, far * own : (far + 1) * own], part[...], ((1,), (0,)))
    out[...] = total


def update(weights, ens):
    own, params = ens[0].shape
    steps = 4 if params % (4 * LANE) == 0 else 1
    block = pl.BlockSpec((own, params // steps), lambda i: (0, i))
    return pl.pallas_call(
        update_kernel,
        grid=(steps,),
        out_shape=jax.ShapeDtypeStruct((own, params), f32),
        in_specs=[pl.BlockSpec(weights.shape, lambda i: (0, 0))] + [block] * len(ens),
        out_specs=block,
        cost_estimate=pl.CostEstimate(
            flops=2 * own * weights.shape[1] * params, bytes_accessed=4 * params * (own + weights.shape[1]), transcendentals=0
        ),
        compiler_params=pltpu.CompilerParams(vmem_limit_bytes=VMEM_LIMIT),
        name="update",
    )(weights, *ens)


def per_device(n_mem, n_par, operator, ensemble, noise, observations, variances, rows):
    index = lax.axis_index("par")
    side = lax.bitwise_and(lax.shift_right_logical(index, 1), 1)

    def swap(x, far, near):
        pairs = [
            (m * n_par + p, (m ^ far) * n_par + (p ^ near)) for m in range(n_mem) for p in range(n_par)
        ]
        return lax.ppermute(x, ("mem", "par"), pairs)

    ens = [ensemble] + [swap(ensemble, far, 0) for far in range(1, n_mem)]
    keep, send = forward(ensemble, operator)
    part = keep + swap(send, 0, 1)
    size = part.shape[0] // 2
    total = lax.dynamic_slice_in_dim(part, side * size, size, 0) + swap(
        lax.dynamic_slice_in_dim(part, (1 - side) * size, size, 0), 0, 2
    )
    target, inverse_var = lookup(rows, observations, variances, noise)
    stride = 4
    while stride < n_par:
        ways = min(4, n_par // stride)
        terms = [total] + [swap(total, 0, d * stride) for d in range(1, ways)]
        if stride == 4:
            terms, target, inverse_var = lax.optimization_barrier((terms, target, inverse_var))
        total = add_all(terms)
        stride *= ways
    places = [(far, dy, 0) for far in range(n_mem) for dy in range(2)]
    pieces = [total if (far, dy) == (0, 0) else swap(total, far, 2 * dy) for far, dy, _ in places]
    pieces += [swap(piece, 0, 1) for piece in pieces]
    places += [(far, dy, 1) for far, dy, _ in places]
    members = ensemble.shape[0] * n_mem
    weights = solve(pieces, places, target, inverse_var, members)
    return update(weights, ens)


def solution(mesh):
    return jax.shard_map(
        functools.partial(per_device, mesh.shape["mem"], mesh.shape["par"]),
        mesh=mesh,
        in_specs=(P("par", None), P("mem", "par"), P("mem", None), P(), P(), P()),
        out_specs=P("mem", "par"),
        check_vma=False,
    )
```

```python
import functools

import jax
import jax.numpy as jnp
from jax import lax
from jax.experimental import pallas as pl
from jax.experimental.pallas import tpu as pltpu
from jax.sharding import PartitionSpec as P

f32 = jnp.float32
HIGHEST = lax.Precision.HIGHEST
SUB, LANE = 8, 128
VMEM = pl.BlockSpec(memory_space=pltpu.VMEM)
HBM = pl.BlockSpec(memory_space=pltpu.HBM)
VMEM_LIMIT = 20 << 20
PARTS, EARLY = 8, 3


def dot(a, b, dims, precision=HIGHEST):
    return lax.dot_general(a, b, (dims, ((), ())), precision=precision, preferred_element_type=f32)


def add_all(terms):
    terms = list(terms)
    while len(terms) > 1:
        pairs = [terms[i] + terms[i + 1] for i in range(0, len(terms) - 1, 2)]
        terms = pairs + ([terms[-1]] if len(terms) % 2 else [])
    return terms[0]


def small_inverse(e):
    n = len(e)

    def at(m, i, k):
        return m[min(i, k)][max(i, k)]

    if n == 2:
        a, b, c = e[0][0], e[0][1], e[1][1]
        d = 1.0 / (a * c - b * b)
        return [[c * d, -(b * d)], [None, a * d]]
    m = n // 2
    span = range(m)
    top = small_inverse([[at(e, i, k) for k in span] for i in span])
    side = [[at(e, i, m + k) for k in span] for i in span]
    t = [[add_all(at(top, i, l) * side[l][k] for l in span) for k in span] for i in span]
    rest = [
        [at(e, m + i, m + k) - add_all(side[l][i] * t[l][k] for l in span) if i <= k else None for k in span]
        for i in span
    ]
    low = small_inverse(rest)
    u = [[add_all(t[i][l] * at(low, l, k) for l in span) for k in span] for i in span]
    out = [[None] * n for _ in range(n)]
    for i in span:
        for k in span:
            if i <= k:
                out[i][k] = top[i][k] + add_all(u[i][l] * t[k][l] for l in span)
                out[m + i][m + k] = low[i][k]
            out[i][m + k] = -u[i][k]
    return out


def across(v, k):
    return jnp.broadcast_to(v[:, k : k + 1], v.shape)


def down(v, i):
    return jnp.broadcast_to(v[i : i + 1, :], v.shape)


def block_inverse(matrix):
    lane = lax.broadcasted_iota(jnp.int32, (SUB, LANE), 1)
    sub = lax.broadcasted_iota(jnp.int32, (SUB, LANE), 0)
    n = LANE // SUB
    m = [matrix[SUB * i : SUB * (i + 1), :] for i in range(n)]
    for j in range(n):
        at = SUB * j
        here = (lane >= at) & (lane < at + SUB)
        cols = [across(m[j], at + k) for k in range(SUB)]
        inv = small_inverse([[down(cols[k], i) if i <= k else None for k in range(SUB)] for i in range(SUB)])
        row = jnp.where(here, (lane - at == sub).astype(f32), m[j])
        rows = [down(row, k) for k in range(SUB)]
        new = [add_all(inv[min(i, k)][max(i, k)] * rows[k] for k in range(SUB)) for i in range(SUB)]
        for d in range(1, n):
            i = (j + d) % n
            drop = add_all(across(m[i], at + k) * new[k] for k in range(SUB))
            m[i] = jnp.where(here, 0.0, m[i]) - drop
        done = new[0]
        for i in range(1, SUB):
            done = jnp.where(sub == i, new[i], done)
        m[j] = done
    return jnp.concatenate(m, axis=0)


def own_bits():
    index = lax.axis_index("par")
    return lax.bitwise_and(index, 1), lax.bitwise_and(lax.shift_right_logical(index, 1), 1)


def dot3(a, b, dims):
    parts = []
    for x in (a, b):
        high = x.astype(jnp.bfloat16)
        parts.append((high, (x - high.astype(f32)).astype(jnp.bfloat16)))
    (ah, al), (bh, bl) = parts
    mul = lambda x, y: lax.dot_general(x, y, (dims, ((), ())), preferred_element_type=f32)
    return mul(ah, bh) + (mul(ah, bl) + mul(al, bh))


def own_bits():
    index = lax.axis_index("par")
    return lax.bitwise_and(index, 1), lax.bitwise_and(lax.shift_right_logical(index, 1), 1)


def forward_kernel(steps, ens, op, keep, send, ens_buf, op_buf, acc, sems):
    depth = op.shape[0] // steps
    cut = lambda i: pl.ds(i * depth, depth)
    copies = [pltpu.make_async_copy(ens, ens_buf, sems.at[steps])]
    copies += [pltpu.make_async_copy(op.at[cut(i), :], op_buf.at[cut(i), :], sems.at[i]) for i in range(steps)]
    for copy in copies:
        copy.start()
    copies[0].wait()
    total = None
    for i in range(steps):
        copies[i + 1].wait()
        term = dot3(ens_buf[:, cut(i)], op_buf[cut(i), :], ((1,), (0,)))
        total = term if total is None else total + term
    acc[...] = total
    half = keep.shape[0]
    core, _ = own_bits()
    keep[...] = acc[pl.ds(pl.multiple_of(core * half, SUB), half), :]
    send[...] = acc[pl.ds(pl.multiple_of((1 - core) * half, SUB), half), :]


def forward(ens, op):
    members, params = ens.shape
    rows = op.shape[1]
    steps = 8 if params % (8 * LANE) == 0 else 1
    half = jax.ShapeDtypeStruct((members // 2, rows), f32)
    return pl.pallas_call(
        functools.partial(forward_kernel, steps),
        out_shape=(half, half),
        in_specs=[HBM, HBM],
        out_specs=(VMEM, VMEM),
        scratch_shapes=[
            pltpu.VMEM(ens.shape, f32),
            pltpu.VMEM(op.shape, f32),
            pltpu.VMEM((members, rows), f32),
            pltpu.SemaphoreType.DMA((steps + 1,)),
        ],
        cost_estimate=pl.CostEstimate(
            flops=2 * members * params * rows, bytes_accessed=4 * (members * params + params * rows), transcendentals=0
        ),
        compiler_params=pltpu.CompilerParams(vmem_limit_bytes=VMEM_LIMIT),
        name="forward",
    )(pltpu.with_memory_space_constraint(ens, pltpu.HBM), pltpu.with_memory_space_constraint(op, pltpu.HBM))


def lookup_kernel(rows, obs, var, noise, target, inverse_var):
    index = rows[...]
    high = lax.shift_right_logical(index, 7)
    low = lax.bitwise_and(index, LANE - 1)
    count = index.shape[1]
    blocks = obs.shape[0]
    pick_high = (lax.broadcasted_iota(jnp.int32, (blocks, count), 0) == high).astype(f32)
    pick_low = (lax.broadcasted_iota(jnp.int32, (LANE, count), 0) == low).astype(f32)
    obs_rows = jnp.sum(dot(obs[...], pick_high, ((0,), (0,))) * pick_low, axis=0, keepdims=True)
    var_rows = jnp.sum(dot(var[...], pick_high, ((0,), (0,))) * pick_low, axis=0, keepdims=True)
    target[...] = obs_rows + jnp.sqrt(var_rows) * noise[...]
    inverse_var[...] = jnp.broadcast_to(1.0 / var_rows, inverse_var.shape)


def lookup(rows, obs, var, noise):
    count = rows.shape[0]
    return pl.pallas_call(
        lookup_kernel,
        out_shape=(
            jax.ShapeDtypeStruct(noise.shape, f32),
            jax.ShapeDtypeStruct((SUB, count), f32),
        ),
        in_specs=[VMEM] * 4,
        out_specs=(VMEM, VMEM),
        cost_estimate=pl.CostEstimate(flops=2 * obs.shape[0] * LANE * count * 12, bytes_accessed=1 << 20, transcendentals=0),
        compiler_params=pltpu.CompilerParams(vmem_limit_bytes=VMEM_LIMIT),
        name="lookup",
    )(rows.reshape(1, count), obs.reshape(-1, LANE), var.reshape(-1, LANE), noise)


def solve_kernel(places, own, *refs):
    own_core, own_side = own_bits()
    count = len(places)
    pieces = refs[:count]
    target, inverse_var = refs[count : count + 2]
    weights = refs[count + 2]
    fwd = refs[count + 3]
    rows = pieces[0].shape[0]
    for piece, (far, dy, dc) in zip(pieces, places):
        core = own_core if dc == 0 else 1 - own_core
        side = own_side if dy == 0 else 1 - own_side
        fwd[pl.ds(pl.multiple_of(far * own + (core * 2 + side) * rows, SUB), rows), :] = piece[...]
    members = fwd.shape[0]
    spread = fwd[...] - jnp.mean(fwd[...], axis=0, keepdims=True)
    weighted = spread * inverse_var[0:1, :]
    gram = dot(weighted, spread, ((1,), (1,)))
    cross = dot(weighted, target[...] - fwd[0:own, :], ((1,), (1,)))
    blocks = members // LANE
    eye = (
        lax.broadcasted_iota(jnp.int32, (LANE, LANE), 0) == lax.broadcasted_iota(jnp.int32, (LANE, LANE), 1)
    ).astype(f32) * (members - 1)
    cut = lambda i: slice(i * LANE, (i + 1) * LANE)
    g = [[gram[cut(i), cut(k)] + (eye if i == k else 0.0) for k in range(blocks)] for i in range(blocks)]
    c = [cross[cut(i), :] for i in range(blocks)]
    t = [[None] * blocks for _ in range(blocks)]
    for j in range(blocks):
        inv = block_inverse(g[j][j])
        c[j] = dot(inv, c[j], ((1,), (0,)))
        for k in range(j + 1, blocks):
            t[j][k] = dot(inv, g[j][k], ((1,), (0,)))
        for i in range(j + 1, blocks):
            c[i] = c[i] - dot(g[i][j], c[j], ((1,), (0,)))
            for k in range(j + 1, blocks):
                g[i][k] = g[i][k] - dot(g[i][j], t[j][k], ((1,), (0,)))
    for j in reversed(range(blocks)):
        for k in range(j + 1, blocks):
            c[j] = c[j] - dot(t[j][k], c[k], ((1,), (0,)))
    w = jnp.concatenate(c, axis=0)
    weights[...] = (w - jnp.mean(w, axis=0, keepdims=True)).T


def solve(pieces, places, target, inverse_var, members):
    own, rows = target.shape
    return pl.pallas_call(
        functools.partial(solve_kernel, places, own),
        out_shape=jax.ShapeDtypeStruct((own, members), f32),
        in_specs=[VMEM] * (len(pieces) + 2),
        out_specs=VMEM,
        scratch_shapes=[pltpu.VMEM((members, rows), f32)],
        cost_estimate=pl.CostEstimate(flops=1, bytes_accessed=1, transcendentals=0),
        compiler_params=pltpu.CompilerParams(vmem_limit_bytes=VMEM_LIMIT),
        name="solve",
    )(*pieces, target, inverse_var)


def update_kernel(fars, weights, own_ens, *refs):
    halves = refs[: 2 * fars]
    out, buf, sems = refs[2 * fars :]
    own, params = own_ens.shape
    steps = sems.shape[0]
    width = params // steps
    copies = []
    for i in range(steps):
        cols = slice(i * width, (i + 1) * width)
        half, at = (0, i) if i * width < halves[0].shape[1] else (1, i - halves[0].shape[1] // width)
        part = own_ens[:, cols]
        total = part + dot3(weights[:, :own], part, ((1,), (0,)))
        for far in range(fars):
            w = weights[:, (far + 1) * own : (far + 2) * own]
            total = total + dot3(w, halves[2 * far + half][:, at * width : (at + 1) * width], ((1,), (0,)))
        buf[:, cols] = total
        copies.append(pltpu.make_async_copy(buf.at[:, cols], out.at[:, cols], sems.at[i]))
        copies[-1].start()
    for copy in copies:
        copy.wait()


def update(weights, own_ens, halves):
    own, params = own_ens.shape
    steps = PARTS
    return pl.pallas_call(
        functools.partial(update_kernel, len(halves) // 2),
        out_shape=jax.ShapeDtypeStruct((own, params), f32),
        in_specs=[VMEM] * (2 + len(halves)),
        out_specs=HBM,
        scratch_shapes=[pltpu.VMEM((own, params), f32), pltpu.SemaphoreType.DMA((steps,))],
        cost_estimate=pl.CostEstimate(
            flops=2 * own * weights.shape[1] * params, bytes_accessed=4 * params * (own + weights.shape[1]), transcendentals=0
        ),
        compiler_params=pltpu.CompilerParams(vmem_limit_bytes=VMEM_LIMIT),
        name="update",
    )(weights, own_ens, *halves)


def per_device(n_mem, n_par, operator, ensemble, noise, observations, variances, rows):
    index = lax.axis_index("par")
    side = lax.bitwise_and(lax.shift_right_logical(index, 1), 1)

    def swap(x, far, near):
        pairs = [
            (m * n_par + p, (m ^ far) * n_par + (p ^ near)) for m in range(n_mem) for p in range(n_par)
        ]
        return lax.ppermute(x, ("mem", "par"), pairs)

    mid = ensemble.shape[1] // PARTS * EARLY
    early = [swap(ensemble[:, :mid], far, 0) for far in range(1, n_mem)]
    keep, send = forward(ensemble, operator)
    part = keep + swap(send, 0, 1)
    size = part.shape[0] // 2
    total = lax.dynamic_slice_in_dim(part, side * size, size, 0) + swap(
        lax.dynamic_slice_in_dim(part, (1 - side) * size, size, 0), 0, 2
    )
    target, inverse_var = lookup(rows, observations, variances, noise)
    stride = 4
    while stride < n_par:
        ways = min(4, n_par // stride)
        terms = [total] + [swap(total, 0, d * stride) for d in range(1, ways)]
        if stride == 4:
            terms, target, inverse_var, early = lax.optimization_barrier((terms, target, inverse_var, early))
        total = add_all(terms)
        stride *= ways
    places = [(far, dy, 0) for far in range(n_mem) for dy in range(2)]
    pieces = [total if (far, dy) == (0, 0) else swap(total, far, 2 * dy) for far, dy, _ in places]
    rest, pieces = lax.optimization_barrier((ensemble[:, mid:], pieces))
    late = [swap(rest, far, 0) for far in range(1, n_mem)]
    pieces += [swap(piece, 0, 1) for piece in pieces]
    places += [(far, dy, 1) for far, dy, _ in places]
    members = ensemble.shape[0] * n_mem
    weights = solve(pieces, places, target, inverse_var, members)
    return update(weights, ensemble, [half for pair in zip(early, late) for half in pair])


def solution(mesh):
    return jax.shard_map(
        functools.partial(per_device, mesh.shape["mem"], mesh.shape["par"]),
        mesh=mesh,
        in_specs=(P("par", None), P("mem", "par"), P("mem", None), P(), P(), P()),
        out_specs=P("mem", "par"),
        check_vma=False,
    )
```

```python
import functools

import jax
import jax.numpy as jnp
from jax import lax
from jax.experimental import pallas as pl
from jax.experimental.pallas import tpu as pltpu
from jax.sharding import PartitionSpec as P

f32 = jnp.float32
HIGHEST = lax.Precision.HIGHEST
SUB, LANE = 8, 128
VMEM = pl.BlockSpec(memory_space=pltpu.VMEM)
HBM = pl.BlockSpec(memory_space=pltpu.HBM)
VMEM_LIMIT = 20 << 20
PARTS, EARLY = 8, 3


def dot(a, b, dims, precision=HIGHEST):
    return lax.dot_general(a, b, (dims, ((), ())), precision=precision, preferred_element_type=f32)


def add_all(terms):
    terms = list(terms)
    while len(terms) > 1:
        pairs = [terms[i] + terms[i + 1] for i in range(0, len(terms) - 1, 2)]
        terms = pairs + ([terms[-1]] if len(terms) % 2 else [])
    return terms[0]


def small_inverse(e):
    n = len(e)

    def at(m, i, k):
        return m[min(i, k)][max(i, k)]

    if n == 2:
        a, b, c = e[0][0], e[0][1], e[1][1]
        d = 1.0 / (a * c - b * b)
        return [[c * d, -(b * d)], [None, a * d]]
    m = n // 2
    span = range(m)
    top = small_inverse([[at(e, i, k) for k in span] for i in span])
    side = [[at(e, i, m + k) for k in span] for i in span]
    t = [[add_all(at(top, i, l) * side[l][k] for l in span) for k in span] for i in span]
    rest = [
        [at(e, m + i, m + k) - add_all(side[l][i] * t[l][k] for l in span) if i <= k else None for k in span]
        for i in span
    ]
    low = small_inverse(rest)
    u = [[add_all(t[i][l] * at(low, l, k) for l in span) for k in span] for i in span]
    out = [[None] * n for _ in range(n)]
    for i in span:
        for k in span:
            if i <= k:
                out[i][k] = top[i][k] + add_all(u[i][l] * t[k][l] for l in span)
                out[m + i][m + k] = low[i][k]
            out[i][m + k] = -u[i][k]
    return out


def across(v, k):
    return jnp.broadcast_to(v[:, k : k + 1], v.shape)


def down(v, i):
    return jnp.broadcast_to(v[i : i + 1, :], v.shape)


def block_inverse(matrix):
    lane = lax.broadcasted_iota(jnp.int32, (SUB, LANE), 1)
    sub = lax.broadcasted_iota(jnp.int32, (SUB, LANE), 0)
    n = LANE // SUB
    m = [matrix[SUB * i : SUB * (i + 1), :] for i in range(n)]
    for j in range(n):
        at = SUB * j
        here = (lane >= at) & (lane < at + SUB)
        cols = [across(m[j], at + k) for k in range(SUB)]
        inv = small_inverse([[down(cols[k], i) if i <= k else None for k in range(SUB)] for i in range(SUB)])
        row = jnp.where(here, (lane - at == sub).astype(f32), m[j])
        rows = [down(row, k) for k in range(SUB)]
        new = [add_all(inv[min(i, k)][max(i, k)] * rows[k] for k in range(SUB)) for i in range(SUB)]
        for d in range(1, n):
            i = (j + d) % n
            drop = add_all(across(m[i], at + k) * new[k] for k in range(SUB))
            m[i] = jnp.where(here, 0.0, m[i]) - drop
        done = new[0]
        for i in range(1, SUB):
            done = jnp.where(sub == i, new[i], done)
        m[j] = done
    return jnp.concatenate(m, axis=0)


def own_bits():
    index = lax.axis_index("par")
    return lax.bitwise_and(index, 1), lax.bitwise_and(lax.shift_right_logical(index, 1), 1)


def dot3(a, b, dims):
    parts = []
    for x in (a, b):
        high = x.astype(jnp.bfloat16)
        parts.append((high, (x - high.astype(f32)).astype(jnp.bfloat16)))
    (ah, al), (bh, bl) = parts
    mul = lambda x, y: lax.dot_general(x, y, (dims, ((), ())), preferred_element_type=f32)
    return mul(ah, bh) + (mul(ah, bl) + mul(al, bh))


def own_bits():
    index = lax.axis_index("par")
    return lax.bitwise_and(index, 1), lax.bitwise_and(lax.shift_right_logical(index, 1), 1)


def forward_kernel(steps, ens, op, keep, send, ens_buf, op_buf, acc, sems):
    depth = op.shape[0] // steps
    cut = lambda i: pl.ds(i * depth, depth)
    copies = [pltpu.make_async_copy(ens, ens_buf, sems.at[steps])]
    copies += [pltpu.make_async_copy(op.at[cut(i), :], op_buf.at[cut(i), :], sems.at[i]) for i in range(steps)]
    for copy in copies:
        copy.start()
    copies[0].wait()
    total = None
    for i in range(steps):
        copies[i + 1].wait()
        term = dot3(ens_buf[:, cut(i)], op_buf[cut(i), :], ((1,), (0,)))
        total = term if total is None else total + term
    acc[...] = total
    half = keep.shape[0]
    core, _ = own_bits()
    keep[...] = acc[pl.ds(pl.multiple_of(core * half, SUB), half), :]
    send[...] = acc[pl.ds(pl.multiple_of((1 - core) * half, SUB), half), :]


def forward(ens, op):
    members, params = ens.shape
    rows = op.shape[1]
    steps = 8 if params % (8 * LANE) == 0 else 1
    half = jax.ShapeDtypeStruct((members // 2, rows), f32)
    return pl.pallas_call(
        functools.partial(forward_kernel, steps),
        out_shape=(half, half),
        in_specs=[HBM, HBM],
        out_specs=(VMEM, VMEM),
        scratch_shapes=[
            pltpu.VMEM(ens.shape, f32),
            pltpu.VMEM(op.shape, f32),
            pltpu.VMEM((members, rows), f32),
            pltpu.SemaphoreType.DMA((steps + 1,)),
        ],
        cost_estimate=pl.CostEstimate(
            flops=2 * members * params * rows, bytes_accessed=4 * (members * params + params * rows), transcendentals=0
        ),
        compiler_params=pltpu.CompilerParams(vmem_limit_bytes=VMEM_LIMIT),
        name="forward",
    )(pltpu.with_memory_space_constraint(ens, pltpu.HBM), pltpu.with_memory_space_constraint(op, pltpu.HBM))


def lookup_kernel(rows, obs, var, noise, target, inverse_var):
    index = rows[...]
    high = lax.shift_right_logical(index, 7)
    low = lax.bitwise_and(index, LANE - 1)
    count = index.shape[1]
    blocks = obs.shape[0]
    pick_high = (lax.broadcasted_iota(jnp.int32, (blocks, count), 0) == high).astype(f32)
    pick_low = (lax.broadcasted_iota(jnp.int32, (LANE, count), 0) == low).astype(f32)
    obs_rows = jnp.sum(dot(obs[...], pick_high, ((0,), (0,))) * pick_low, axis=0, keepdims=True)
    var_rows = jnp.sum(dot(var[...], pick_high, ((0,), (0,))) * pick_low, axis=0, keepdims=True)
    target[...] = obs_rows + jnp.sqrt(var_rows) * noise[...]
    inverse_var[...] = jnp.broadcast_to(1.0 / var_rows, inverse_var.shape)


def lookup(rows, obs, var, noise):
    count = rows.shape[0]
    return pl.pallas_call(
        lookup_kernel,
        out_shape=(
            jax.ShapeDtypeStruct(noise.shape, f32),
            jax.ShapeDtypeStruct((SUB, count), f32),
        ),
        in_specs=[VMEM] * 4,
        out_specs=(VMEM, VMEM),
        cost_estimate=pl.CostEstimate(flops=2 * obs.shape[0] * LANE * count * 12, bytes_accessed=1 << 20, transcendentals=0),
        compiler_params=pltpu.CompilerParams(vmem_limit_bytes=VMEM_LIMIT),
        name="lookup",
    )(rows.reshape(1, count), obs.reshape(-1, LANE), var.reshape(-1, LANE), noise)


def solve_kernel(places, own, *refs):
    count = len(places)
    pieces = refs[:count]
    target, inverse_var, weights, fwd, gram, cross, inverse = refs[count:]
    own_core, own_side = own_bits()
    rows = pieces[0].shape[0]
    for piece, (far, dy, dc) in zip(pieces, places):
        core = own_core if dc == 0 else 1 - own_core
        side = own_side if dy == 0 else 1 - own_side
        fwd[pl.ds(pl.multiple_of(far * own + (core * 2 + side) * rows, SUB), rows), :] = piece[...]
    members = fwd.shape[0]
    spread = fwd[...] - jnp.mean(fwd[...], axis=0, keepdims=True)
    weighted = spread * inverse_var[0:1, :]
    row = lax.broadcasted_iota(jnp.int32, gram.shape, 0)
    col = lax.broadcasted_iota(jnp.int32, gram.shape, 1)
    gram[...] = dot3(weighted, spread, ((1,), (1,))) + jnp.where(row == col, float(members - 1), 0.0)
    cross[...] = dot3(weighted, target[...] - fwd[0:own, :], ((1,), (1,)))
    blocks = members // LANE
    cut = lambda i: slice(i * LANE, (i + 1) * LANE)

    def eliminate(j, carry):
        at = pl.ds(pl.multiple_of(j * LANE, LANE), LANE)
        inverse[...] = block_inverse(gram[at, at])
        for i in range(blocks):

            @pl.when(j == i)
            def _():
                top = dot3(inverse[...], cross[cut(i), :], ((1,), (0,)))
                cross[cut(i), :] = top
                if i + 1 < blocks:
                    rest = slice((i + 1) * LANE, members)
                    low = gram[rest, cut(i)]
                    side = dot3(inverse[...], gram[cut(i), rest], ((1,), (0,)))
                    gram[rest, rest] = gram[rest, rest] - dot3(low, side, ((1,), (0,)))
                    cross[rest, :] = cross[rest, :] - dot3(low, top, ((1,), (0,)))
                    gram[cut(i), rest] = side

        return carry

    lax.fori_loop(0, blocks, eliminate, 0)
    for i in reversed(range(blocks - 1)):
        rest = slice((i + 1) * LANE, members)
        cross[cut(i), :] = cross[cut(i), :] - dot3(gram[cut(i), rest], cross[rest, :], ((1,), (0,)))
    w = cross[...]
    weights[...] = (w - jnp.mean(w, axis=0, keepdims=True)).T


def solve(pieces, places, target, inverse_var, members):
    own, rows = target.shape
    return pl.pallas_call(
        functools.partial(solve_kernel, places, own),
        out_shape=jax.ShapeDtypeStruct((own, members), f32),
        in_specs=[VMEM] * (len(pieces) + 2),
        out_specs=VMEM,
        scratch_shapes=[
            pltpu.VMEM((members, rows), f32),
            pltpu.VMEM((members, members), f32),
            pltpu.VMEM((members, own), f32),
            pltpu.VMEM((LANE, LANE), f32),
        ],
        cost_estimate=pl.CostEstimate(flops=6_000_000_000, bytes_accessed=1, transcendentals=0),
        compiler_params=pltpu.CompilerParams(vmem_limit_bytes=VMEM_LIMIT),
        name="solve",
    )(*pieces, target, inverse_var)


def update_kernel(fars, weights, own_ens, *refs):
    halves = refs[: 2 * fars]
    out, buf, sems = refs[2 * fars :]
    own, params = own_ens.shape
    steps = sems.shape[0]
    width = params // steps
    copies = []
    for i in range(steps):
        cols = slice(i * width, (i + 1) * width)
        half, at = (0, i) if i * width < halves[0].shape[1] else (1, i - halves[0].shape[1] // width)
        part = own_ens[:, cols]
        total = part + dot3(weights[:, :own], part, ((1,), (0,)))
        for far in range(fars):
            w = weights[:, (far + 1) * own : (far + 2) * own]
            total = total + dot3(w, halves[2 * far + half][:, at * width : (at + 1) * width], ((1,), (0,)))
        buf[:, cols] = total
        copies.append(pltpu.make_async_copy(buf.at[:, cols], out.at[:, cols], sems.at[i]))
        copies[-1].start()
    for copy in copies:
        copy.wait()


def update(weights, own_ens, halves):
    own, params = own_ens.shape
    steps = PARTS
    return pl.pallas_call(
        functools.partial(update_kernel, len(halves) // 2),
        out_shape=jax.ShapeDtypeStruct((own, params), f32),
        in_specs=[VMEM] * (2 + len(halves)),
        out_specs=HBM,
        scratch_shapes=[pltpu.VMEM((own, params), f32), pltpu.SemaphoreType.DMA((steps,))],
        cost_estimate=pl.CostEstimate(
            flops=2 * own * weights.shape[1] * params, bytes_accessed=4 * params * (own + weights.shape[1]), transcendentals=0
        ),
        compiler_params=pltpu.CompilerParams(vmem_limit_bytes=VMEM_LIMIT),
        name="update",
    )(weights, own_ens, *halves)


def per_device(n_mem, n_par, operator, ensemble, noise, observations, variances, rows):
    index = lax.axis_index("par")
    side = lax.bitwise_and(lax.shift_right_logical(index, 1), 1)

    def swap(x, far, near):
        pairs = [
            (m * n_par + p, (m ^ far) * n_par + (p ^ near)) for m in range(n_mem) for p in range(n_par)
        ]
        return lax.ppermute(x, ("mem", "par"), pairs)

    mid = ensemble.shape[1] // PARTS * EARLY
    early = [swap(ensemble[:, :mid], far, 0) for far in range(1, n_mem)]
    keep, send = forward(ensemble, operator)
    part = keep + swap(send, 0, 1)
    size = part.shape[0] // 2
    total = lax.dynamic_slice_in_dim(part, side * size, size, 0) + swap(
        lax.dynamic_slice_in_dim(part, (1 - side) * size, size, 0), 0, 2
    )
    target, inverse_var = lookup(rows, observations, variances, noise)
    stride = 4
    while stride < n_par:
        ways = min(4, n_par // stride)
        terms = [total] + [swap(total, 0, d * stride) for d in range(1, ways)]
        if stride == 4:
            terms, target, inverse_var, early = lax.optimization_barrier((terms, target, inverse_var, early))
        total = add_all(terms)
        stride *= ways
    places = [(far, dy, 0) for far in range(n_mem) for dy in range(2)]
    pieces = [total if (far, dy) == (0, 0) else swap(total, far, 2 * dy) for far, dy, _ in places]
    rest, _ = lax.optimization_barrier((ensemble[:, mid:], total))
    late = [swap(rest, far, 0) for far in range(1, n_mem)]
    pieces += [swap(piece, 0, 1) for piece in pieces]
    places += [(far, dy, 1) for far, dy, _ in places]
    members = ensemble.shape[0] * n_mem
    weights = solve(pieces, places, target, inverse_var, members)
    return update(weights, ensemble, [half for pair in zip(early, late) for half in pair])


def solution(mesh):
    return jax.shard_map(
        functools.partial(per_device, mesh.shape["mem"], mesh.shape["par"]),
        mesh=mesh,
        in_specs=(P("par", None), P("mem", "par"), P("mem", None), P(), P(), P()),
        out_specs=P("mem", "par"),
        check_vma=False,
    )
```

```python
import functools

import jax
import jax.numpy as jnp
from jax import lax
from jax.experimental import pallas as pl
from jax.experimental.pallas import tpu as pltpu
from jax.sharding import PartitionSpec as P

f32 = jnp.float32
HIGHEST = lax.Precision.HIGHEST
SUB, LANE = 8, 128
VMEM = pl.BlockSpec(memory_space=pltpu.VMEM)
HBM = pl.BlockSpec(memory_space=pltpu.HBM)
VMEM_LIMIT = 20 << 20
PARTS, EARLY = 8, 3


def dot(a, b, dims, precision=HIGHEST):
    return lax.dot_general(a, b, (dims, ((), ())), precision=precision, preferred_element_type=f32)


def add_all(terms):
    terms = list(terms)
    while len(terms) > 1:
        pairs = [terms[i] + terms[i + 1] for i in range(0, len(terms) - 1, 2)]
        terms = pairs + ([terms[-1]] if len(terms) % 2 else [])
    return terms[0]


def pivot_rows(e, rows):
    n = len(rows)
    e = [list(line) for line in e]
    rows = list(rows)
    low = [[None] * n for _ in range(n)]
    out = [None] * n
    for a in range(0, n, 2):
        b = a + 1
        scale = 1.0 / (e[a][a] * e[b][b] - e[a][b] * e[a][b])
        aa, bb, ab = e[b][b] * scale, e[a][a] * scale, -(e[a][b] * scale)
        out[a] = aa * rows[a] + ab * rows[b]
        out[b] = ab * rows[a] + bb * rows[b]
        for i in range(b + 1, n):
            la = e[a][i] * aa + e[b][i] * ab
            lb = e[a][i] * ab + e[b][i] * bb
            low[i][a], low[i][b] = la, lb
            for m in range(i, n):
                e[i][m] = e[i][m] - (la * e[a][m] + lb * e[b][m])
            rows[i] = rows[i] - (la * rows[a] + lb * rows[b])
    for a in range(n - 4, -1, -2):
        for k in (a, a + 1):
            out[k] = out[k] - add_all(low[i][k] * out[i] for i in range(a + 2, n))
    return out


def across(v, k):
    return jnp.broadcast_to(v[:, k : k + 1], v.shape)


def block_inverse(matrix, buf):
    size = matrix.shape[0]
    lane = lax.broadcasted_iota(jnp.int32, (SUB, size), 1)
    sub = lax.broadcasted_iota(jnp.int32, (SUB, size), 0)
    n = size // SUB
    m = [matrix[SUB * i : SUB * (i + 1), :] for i in range(n)]
    low, scaled = [], []
    for j in range(n):
        at = SUB * j
        here = (lane >= at) & (lane < at + SUB)
        base = (j % 2) * SUB * (SUB + 1)
        for k in range(SUB):
            buf[base + SUB * k : base + SUB * (k + 1), :] = across(m[j], at + k)
        row = jnp.where(here, (lane - at == sub).astype(f32), m[j])
        buf[base + SUB * SUB : base + SUB * (SUB + 1), :] = row
        spread = lambda i: jnp.broadcast_to(buf[base + i : base + i + 1, :], (SUB, size))
        e = [[spread(SUB * k + i) if i <= k else None for k in range(SUB)] for i in range(SUB)]
        new = pivot_rows(e, [spread(SUB * SUB + k) for k in range(SUB)])
        for i in range(j + 1, n):
            m[i] = jnp.where(here, 0.0, m[i]) - add_all(across(m[i], at + k) * new[k] for k in range(SUB))
        done = new[0]
        for i in range(1, SUB):
            done = jnp.where(sub == i, new[i], done)
        keep = lane < at + SUB
        low.append(jnp.where(keep, row, 0.0))
        scaled.append(jnp.where(keep, done, 0.0))
    return jnp.concatenate(low, axis=0), jnp.concatenate(scaled, axis=0)


def own_bits():
    index = lax.axis_index("par")
    return lax.bitwise_and(index, 1), lax.bitwise_and(lax.shift_right_logical(index, 1), 1)


def dot3(a, b, dims):
    parts = []
    for x in (a, b):
        high = x.astype(jnp.bfloat16)
        parts.append((high, (x - high.astype(f32)).astype(jnp.bfloat16)))
    (ah, al), (bh, bl) = parts
    mul = lambda x, y: lax.dot_general(x, y, (dims, ((), ())), preferred_element_type=f32)
    return mul(ah, bh) + (mul(ah, bl) + mul(al, bh))


def own_bits():
    index = lax.axis_index("par")
    return lax.bitwise_and(index, 1), lax.bitwise_and(lax.shift_right_logical(index, 1), 1)


def forward_kernel(steps, ens, op, keep, send, ens_buf, op_buf, acc, sems):
    depth = op.shape[0] // steps
    cut = lambda i: pl.ds(i * depth, depth)
    copies = [pltpu.make_async_copy(ens, ens_buf, sems.at[steps])]
    copies += [pltpu.make_async_copy(op.at[cut(i), :], op_buf.at[cut(i), :], sems.at[i]) for i in range(steps)]
    for copy in copies:
        copy.start()
    copies[0].wait()
    total = None
    for i in range(steps):
        copies[i + 1].wait()
        term = dot3(ens_buf[:, cut(i)], op_buf[cut(i), :], ((1,), (0,)))
        total = term if total is None else total + term
    acc[...] = total
    half = keep.shape[0]
    core, _ = own_bits()
    keep[...] = acc[pl.ds(pl.multiple_of(core * half, SUB), half), :]
    send[...] = acc[pl.ds(pl.multiple_of((1 - core) * half, SUB), half), :]


def forward(ens, op):
    members, params = ens.shape
    rows = op.shape[1]
    steps = 8 if params % (8 * LANE) == 0 else 1
    half = jax.ShapeDtypeStruct((members // 2, rows), f32)
    return pl.pallas_call(
        functools.partial(forward_kernel, steps),
        out_shape=(half, half),
        in_specs=[HBM, HBM],
        out_specs=(VMEM, VMEM),
        scratch_shapes=[
            pltpu.VMEM(ens.shape, f32),
            pltpu.VMEM(op.shape, f32),
            pltpu.VMEM((members, rows), f32),
            pltpu.SemaphoreType.DMA((steps + 1,)),
        ],
        cost_estimate=pl.CostEstimate(
            flops=2 * members * params * rows, bytes_accessed=4 * (members * params + params * rows), transcendentals=0
        ),
        compiler_params=pltpu.CompilerParams(vmem_limit_bytes=VMEM_LIMIT),
        name="forward",
    )(pltpu.with_memory_space_constraint(ens, pltpu.HBM), pltpu.with_memory_space_constraint(op, pltpu.HBM))


def lookup_kernel(rows, obs, var, noise, target, root):
    index = rows[...]
    high = lax.shift_right_logical(index, 7)
    low = lax.bitwise_and(index, LANE - 1)
    count = index.shape[1]
    blocks = obs.shape[0]
    pick_high = (lax.broadcasted_iota(jnp.int32, (blocks, count), 0) == high).astype(f32)
    pick_low = (lax.broadcasted_iota(jnp.int32, (LANE, count), 0) == low).astype(f32)
    obs_rows = jnp.sum(dot(obs[...], pick_high, ((0,), (0,))) * pick_low, axis=0, keepdims=True)
    var_rows = jnp.sum(dot(var[...], pick_high, ((0,), (0,))) * pick_low, axis=0, keepdims=True)
    target[...] = obs_rows + jnp.sqrt(var_rows) * noise[...]
    root[...] = jnp.broadcast_to(lax.rsqrt(var_rows), root.shape)


def lookup(rows, obs, var, noise):
    count = rows.shape[0]
    return pl.pallas_call(
        lookup_kernel,
        out_shape=(
            jax.ShapeDtypeStruct(noise.shape, f32),
            jax.ShapeDtypeStruct((SUB, count), f32),
        ),
        in_specs=[VMEM] * 4,
        out_specs=(VMEM, VMEM),
        cost_estimate=pl.CostEstimate(flops=2 * obs.shape[0] * LANE * count * 12, bytes_accessed=1 << 20, transcendentals=0),
        compiler_params=pltpu.CompilerParams(vmem_limit_bytes=VMEM_LIMIT),
        name="lookup",
    )(rows.reshape(1, count), obs.reshape(-1, LANE), var.reshape(-1, LANE), noise)


def fenced(body):
    pl.when(lax.axis_index("par") >= 0)(body)


def set_inverse(out, matrix, buf, low, scaled):
    @fenced
    def _():
        low[...], scaled[...] = block_inverse(matrix[...], buf)

    out[...] = dot3(low[...], scaled[...], ((0,), (0,)))


def add_diagonal(matrix, value):
    row = lax.broadcasted_iota(jnp.int32, matrix.shape, 0)
    col = lax.broadcasted_iota(jnp.int32, matrix.shape, 1)
    return matrix + jnp.where(row == col, value, 0.0)


def near_kernel(members, count, *refs):
    pieces = refs[:count]
    root, inverse, near, shift, gram, buf, low, scaled = refs[count:]
    rows = pieces[0].shape[0]
    for i, piece in enumerate(pieces):
        near[i * rows : (i + 1) * rows, :] = piece[...]
    mean = jnp.mean(near[...], axis=0, keepdims=True)
    shift[...] = jnp.broadcast_to(mean, shift.shape)
    z = (near[...] - mean) * root[0:1, :]
    near[...] = z
    gram[...] = add_diagonal(dot3(z, z, ((1,), (1,))), float(members - 1))
    set_inverse(inverse, gram, buf, low, scaled)


def solve_near(pieces, root, members):
    rows, cols = pieces[0].shape
    size = rows * len(pieces)
    square = jax.ShapeDtypeStruct((size, size), f32)
    return pl.pallas_call(
        functools.partial(near_kernel, members, len(pieces)),
        out_shape=(square, jax.ShapeDtypeStruct((size, cols), f32), jax.ShapeDtypeStruct((SUB, cols), f32)),
        in_specs=[VMEM] * (len(pieces) + 1),
        out_specs=(VMEM, VMEM, VMEM),
        scratch_shapes=solve_scratch(size),
        cost_estimate=pl.CostEstimate(flops=3_000_000_000, bytes_accessed=1, transcendentals=0),
        compiler_params=pltpu.CompilerParams(vmem_limit_bytes=VMEM_LIMIT),
        name="solve_near",
    )(*pieces, root)


def solve_scratch(size):
    return [
        pltpu.VMEM((size, size), f32),
        pltpu.VMEM((2 * SUB * (SUB + 1), size), f32),
        pltpu.VMEM((size, size), f32),
        pltpu.VMEM((size, size), f32),
    ]


def solve_kernel(places, *refs):
    count = len(places)
    pieces = refs[:count]
    inverse, near, shift, target, root, weights = refs[count : count + 6]
    fwd, gram, buf, low, scaled, second, far_z, right, out = refs[count + 6 :]
    rows = pieces[0].shape[0]
    own, size = target.shape[0], near.shape[0]
    members = 2 * size
    own_core, own_side = own_bits()

    def start(place):
        far, dy, dc = place
        core = own_core if dc == 0 else 1 - own_core
        side = own_side if dy == 0 else 1 - own_side
        return pl.multiple_of(far * own + (core * 2 + side) * rows, SUB)

    for piece, place in zip(pieces, places):
        if place[0] == 0:
            fwd[pl.ds(start(place), rows), :] = piece[...]
    scale = root[0:1, :]
    for i, piece in enumerate(pieces[count // 2 :]):
        far_z[i * rows : (i + 1) * rows, :] = (piece[...] - shift[0:1, :]) * scale
    residual = (target[...] - fwd[...]) * scale
    za, zb = near[...], far_z[...]
    side = dot3(zb, za, ((1,), (1,)))
    ca, cb = dot3(za, residual, ((1,), (1,))), dot3(zb, residual, ((1,), (1,)))
    mean = (jnp.sum(ca, axis=0, keepdims=True) + jnp.sum(cb, axis=0, keepdims=True)) / members
    ones = jnp.ones((size, own), f32)
    ra = jnp.concatenate([ca - mean, ones], axis=1)
    rb = jnp.concatenate([cb - mean, ones], axis=1)
    top = dot3(inverse[...], jnp.concatenate([side.T, ra], axis=1), ((1,), (0,)))
    drop = dot3(side, top, ((1,), (0,)))
    gram[...] = add_diagonal(dot3(zb, zb, ((1,), (1,))), float(members - 1)) - drop[:, :size]
    right[0:size, :] = top
    right[size:, size:] = rb - drop[:, size:]
    set_inverse(second, gram, buf, low, scaled)
    xb = dot3(second[...], right[size:, size:], ((1,), (0,)))
    xa = right[0:size, size:] - dot3(right[0:size, 0:size], xb, ((1,), (0,)))
    x = jnp.concatenate([xa, xb], axis=0)
    w, unit = x[:, :own], x[:, own:]
    w = w - unit * (jnp.sum(w, axis=0, keepdims=True) / jnp.sum(unit, axis=0, keepdims=True))
    w = w - jnp.mean(w, axis=0, keepdims=True)
    for i, place in enumerate(places):
        out[pl.ds(start(place), rows), :] = w[i * rows : (i + 1) * rows, :]
    weights[...] = out[...].T


def solve(pieces, places, inverse, near, shift, target, root):
    own, cols = target.shape
    size = near.shape[0]
    return pl.pallas_call(
        functools.partial(solve_kernel, places),
        out_shape=jax.ShapeDtypeStruct((own, 2 * size), f32),
        in_specs=[VMEM] * (len(pieces) + 5),
        out_specs=VMEM,
        scratch_shapes=[pltpu.VMEM((own, cols), f32)]
        + solve_scratch(size)
        + [
            pltpu.VMEM((size, size), f32),
            pltpu.VMEM((size, cols), f32),
            pltpu.VMEM((2 * size, size + 2 * own), f32),
            pltpu.VMEM((2 * size, own), f32),
        ],
        cost_estimate=pl.CostEstimate(flops=3_000_000_000, bytes_accessed=1, transcendentals=0),
        compiler_params=pltpu.CompilerParams(vmem_limit_bytes=VMEM_LIMIT),
        name="solve",
    )(*pieces, inverse, near, shift, target, root)


def update_kernel(fars, weights, own_ens, *refs):
    halves = refs[: 2 * fars]
    out, buf, sems = refs[2 * fars :]
    own, params = own_ens.shape
    steps = sems.shape[0]
    width = params // steps
    copies = []
    for i in range(steps):
        cols = slice(i * width, (i + 1) * width)
        half, at = (0, i) if i * width < halves[0].shape[1] else (1, i - halves[0].shape[1] // width)
        part = own_ens[:, cols]
        total = part + dot3(weights[:, :own], part, ((1,), (0,)))
        for far in range(fars):
            w = weights[:, (far + 1) * own : (far + 2) * own]
            total = total + dot3(w, halves[2 * far + half][:, at * width : (at + 1) * width], ((1,), (0,)))
        buf[:, cols] = total
        copies.append(pltpu.make_async_copy(buf.at[:, cols], out.at[:, cols], sems.at[i]))
        copies[-1].start()
    for copy in copies:
        copy.wait()


def update(weights, own_ens, halves):
    own, params = own_ens.shape
    steps = PARTS
    return pl.pallas_call(
        functools.partial(update_kernel, len(halves) // 2),
        out_shape=jax.ShapeDtypeStruct((own, params), f32),
        in_specs=[VMEM] * (2 + len(halves)),
        out_specs=HBM,
        scratch_shapes=[pltpu.VMEM((own, params), f32), pltpu.SemaphoreType.DMA((steps,))],
        cost_estimate=pl.CostEstimate(
            flops=2 * own * weights.shape[1] * params, bytes_accessed=4 * params * (own + weights.shape[1]), transcendentals=0
        ),
        compiler_params=pltpu.CompilerParams(vmem_limit_bytes=VMEM_LIMIT),
        name="update",
    )(weights, own_ens, *halves)


def per_device(n_mem, n_par, operator, ensemble, noise, observations, variances, rows):
    index = lax.axis_index("par")
    side = lax.bitwise_and(lax.shift_right_logical(index, 1), 1)

    def swap(x, far, near):
        pairs = [
            (m * n_par + p, (m ^ far) * n_par + (p ^ near)) for m in range(n_mem) for p in range(n_par)
        ]
        return lax.ppermute(x, ("mem", "par"), pairs)

    mid = ensemble.shape[1] // PARTS * EARLY
    early = [swap(ensemble[:, :mid], far, 0) for far in range(1, n_mem)]
    keep, send = forward(ensemble, operator)
    part = keep + swap(send, 0, 1)
    size = part.shape[0] // 2
    total = lax.dynamic_slice_in_dim(part, side * size, size, 0) + swap(
        lax.dynamic_slice_in_dim(part, (1 - side) * size, size, 0), 0, 2
    )
    target, root = lookup(rows, observations, variances, noise)
    stride = 4
    while stride < n_par:
        ways = min(4, n_par // stride)
        terms = [total] + [swap(total, 0, d * stride) for d in range(1, ways)]
        if stride == 4:
            terms, target, root, early = lax.optimization_barrier((terms, target, root, early))
        total = add_all(terms)
        stride *= ways
    places = [(far, dy, 0) for far in range(n_mem) for dy in range(2)]
    pieces = [total if (far, dy) == (0, 0) else swap(total, far, 2 * dy) for far, dy, _ in places]
    rest, _ = lax.optimization_barrier((ensemble[:, mid:], total))
    late = [swap(rest, far, 0) for far in range(1, n_mem)]
    inverse, near, shift = solve_near(pieces, root, ensemble.shape[0] * n_mem)
    pieces += [swap(piece, 0, 1) for piece in pieces]
    places += [(far, dy, 1) for far, dy, _ in places]
    weights = solve(pieces, places, inverse, near, shift, target, root)
    return update(weights, ensemble, [half for pair in zip(early, late) for half in pair])


def solution(mesh):
    return jax.shard_map(
        functools.partial(per_device, mesh.shape["mem"], mesh.shape["par"]),
        mesh=mesh,
        in_specs=(P("par", None), P("mem", "par"), P("mem", None), P(), P(), P()),
        out_specs=P("mem", "par"),
        check_vma=False,
    )
```

```python
import functools

import jax
import jax.numpy as jnp
from jax import lax
from jax.experimental import pallas as pl
from jax.experimental.pallas import tpu as pltpu
from jax.sharding import PartitionSpec as P

f32 = jnp.float32
HIGHEST = lax.Precision.HIGHEST
SUB, LANE = 8, 128
VMEM = pl.BlockSpec(memory_space=pltpu.VMEM)
HBM = pl.BlockSpec(memory_space=pltpu.HBM)
VMEM_LIMIT = 20 << 20
PARTS = 8
CUTS = (0, 1, 4, 8)


def dot(a, b, dims, precision=HIGHEST):
    return lax.dot_general(a, b, (dims, ((), ())), precision=precision, preferred_element_type=f32)


def add_all(terms):
    terms = list(terms)
    while len(terms) > 1:
        pairs = [terms[i] + terms[i + 1] for i in range(0, len(terms) - 1, 2)]
        terms = pairs + ([terms[-1]] if len(terms) % 2 else [])
    return terms[0]


def pivot_rows(e, rows):
    n = len(rows)
    e = [list(line) for line in e]
    rows = list(rows)
    low = [[None] * n for _ in range(n)]
    out = [None] * n
    for a in range(0, n, 2):
        b = a + 1
        scale = 1.0 / (e[a][a] * e[b][b] - e[a][b] * e[a][b])
        aa, bb, ab = e[b][b] * scale, e[a][a] * scale, -(e[a][b] * scale)
        out[a] = aa * rows[a] + ab * rows[b]
        out[b] = ab * rows[a] + bb * rows[b]
        for i in range(b + 1, n):
            la = e[a][i] * aa + e[b][i] * ab
            lb = e[a][i] * ab + e[b][i] * bb
            low[i][a], low[i][b] = la, lb
            for m in range(i, n):
                e[i][m] = e[i][m] - (la * e[a][m] + lb * e[b][m])
            rows[i] = rows[i] - (la * rows[a] + lb * rows[b])
    for a in range(n - 4, -1, -2):
        for k in (a, a + 1):
            out[k] = out[k] - add_all(low[i][k] * out[i] for i in range(a + 2, n))
    return out


def across(v, k):
    return jnp.broadcast_to(v[:, k : k + 1], v.shape)


def block_inverse(matrix, buf):
    size = matrix.shape[0]
    lane = lax.broadcasted_iota(jnp.int32, (SUB, size), 1)
    sub = lax.broadcasted_iota(jnp.int32, (SUB, size), 0)
    n = size // SUB
    m = [matrix[SUB * i : SUB * (i + 1), :] for i in range(n)]
    low, scaled = [], []
    for j in range(n):
        at = SUB * j
        here = (lane >= at) & (lane < at + SUB)
        base = (j % 2) * SUB * (SUB + 1)
        for k in range(SUB):
            buf[base + SUB * k : base + SUB * (k + 1), :] = across(m[j], at + k)
        row = jnp.where(here, (lane - at == sub).astype(f32), m[j])
        buf[base + SUB * SUB : base + SUB * (SUB + 1), :] = row
        spread = lambda i: jnp.broadcast_to(buf[base + i : base + i + 1, :], (SUB, size))
        e = [[spread(SUB * k + i) if i <= k else None for k in range(SUB)] for i in range(SUB)]
        new = pivot_rows(e, [spread(SUB * SUB + k) for k in range(SUB)])
        for i in range(j + 1, n):
            m[i] = jnp.where(here, 0.0, m[i]) - add_all(across(m[i], at + k) * new[k] for k in range(SUB))
        done = new[0]
        for i in range(1, SUB):
            done = jnp.where(sub == i, new[i], done)
        keep = lane < at + SUB
        low.append(jnp.where(keep, row, 0.0))
        scaled.append(jnp.where(keep, done, 0.0))
    return jnp.concatenate(low, axis=0), jnp.concatenate(scaled, axis=0)


def own_bits():
    index = lax.axis_index("par")
    return lax.bitwise_and(index, 1), lax.bitwise_and(lax.shift_right_logical(index, 1), 1)


def dot3(a, b, dims):
    parts = []
    for x in (a, b):
        high = x.astype(jnp.bfloat16)
        parts.append((high, (x - high.astype(f32)).astype(jnp.bfloat16)))
    (ah, al), (bh, bl) = parts
    mul = lambda x, y: lax.dot_general(x, y, (dims, ((), ())), preferred_element_type=f32)
    return mul(ah, bh) + (mul(ah, bl) + mul(al, bh))


def own_bits():
    index = lax.axis_index("par")
    return lax.bitwise_and(index, 1), lax.bitwise_and(lax.shift_right_logical(index, 1), 1)


def forward_kernel(steps, ens, op, keep, send, ens_buf, op_buf, acc, sems):
    depth = op.shape[0] // steps
    cut = lambda i: pl.ds(i * depth, depth)
    copies = [pltpu.make_async_copy(ens, ens_buf, sems.at[steps])]
    copies += [pltpu.make_async_copy(op.at[cut(i), :], op_buf.at[cut(i), :], sems.at[i]) for i in range(steps)]
    for copy in copies:
        copy.start()
    copies[0].wait()
    total = None
    for i in range(steps):
        copies[i + 1].wait()
        term = dot3(ens_buf[:, cut(i)], op_buf[cut(i), :], ((1,), (0,)))
        total = term if total is None else total + term
    acc[...] = total
    half = keep.shape[0]
    core, _ = own_bits()
    keep[...] = acc[pl.ds(pl.multiple_of(core * half, SUB), half), :]
    send[...] = acc[pl.ds(pl.multiple_of((1 - core) * half, SUB), half), :]


def forward(ens, op):
    members, params = ens.shape
    rows = op.shape[1]
    steps = 8 if params % (8 * LANE) == 0 else 1
    half = jax.ShapeDtypeStruct((members // 2, rows), f32)
    return pl.pallas_call(
        functools.partial(forward_kernel, steps),
        out_shape=(half, half),
        in_specs=[HBM, HBM],
        out_specs=(VMEM, VMEM),
        scratch_shapes=[
            pltpu.VMEM(ens.shape, f32),
            pltpu.VMEM(op.shape, f32),
            pltpu.VMEM((members, rows), f32),
            pltpu.SemaphoreType.DMA((steps + 1,)),
        ],
        cost_estimate=pl.CostEstimate(
            flops=2 * members * params * rows, bytes_accessed=4 * (members * params + params * rows), transcendentals=0
        ),
        compiler_params=pltpu.CompilerParams(vmem_limit_bytes=VMEM_LIMIT),
        name="forward",
    )(pltpu.with_memory_space_constraint(ens, pltpu.HBM), pltpu.with_memory_space_constraint(op, pltpu.HBM))


def lookup_kernel(rows, obs, var, noise, target, root):
    index = rows[...]
    high = lax.shift_right_logical(index, 7)
    low = lax.bitwise_and(index, LANE - 1)
    count = index.shape[1]
    blocks = obs.shape[0]
    pick_high = (lax.broadcasted_iota(jnp.int32, (blocks, count), 0) == high).astype(f32)
    pick_low = (lax.broadcasted_iota(jnp.int32, (LANE, count), 0) == low).astype(f32)
    obs_rows = jnp.sum(dot(obs[...], pick_high, ((0,), (0,))) * pick_low, axis=0, keepdims=True)
    var_rows = jnp.sum(dot(var[...], pick_high, ((0,), (0,))) * pick_low, axis=0, keepdims=True)
    target[...] = obs_rows + jnp.sqrt(var_rows) * noise[...]
    root[...] = jnp.broadcast_to(lax.rsqrt(var_rows), root.shape)


def lookup(rows, obs, var, noise):
    count = rows.shape[0]
    return pl.pallas_call(
        lookup_kernel,
        out_shape=(
            jax.ShapeDtypeStruct(noise.shape, f32),
            jax.ShapeDtypeStruct((SUB, count), f32),
        ),
        in_specs=[VMEM] * 4,
        out_specs=(VMEM, VMEM),
        cost_estimate=pl.CostEstimate(flops=2 * obs.shape[0] * LANE * count * 12, bytes_accessed=1 << 20, transcendentals=0),
        compiler_params=pltpu.CompilerParams(vmem_limit_bytes=VMEM_LIMIT),
        name="lookup",
    )(rows.reshape(1, count), obs.reshape(-1, LANE), var.reshape(-1, LANE), noise)


def fenced(body):
    pl.when(lax.axis_index("par") >= 0)(body)


def set_inverse(out, matrix, buf, low, scaled):
    @fenced
    def _():
        low[...], scaled[...] = block_inverse(matrix[...], buf)

    out[...] = dot3(low[...], scaled[...], ((0,), (0,)))


def add_diagonal(matrix, value):
    row = lax.broadcasted_iota(jnp.int32, matrix.shape, 0)
    col = lax.broadcasted_iota(jnp.int32, matrix.shape, 1)
    return matrix + jnp.where(row == col, value, 0.0)


def near_kernel(members, count, *refs):
    pieces = refs[:count]
    root, inverse, near, shift, gram, buf, low, scaled = refs[count:]
    rows = pieces[0].shape[0]
    for i, piece in enumerate(pieces):
        near[i * rows : (i + 1) * rows, :] = piece[...]
    mean = jnp.mean(near[...], axis=0, keepdims=True)
    shift[...] = jnp.broadcast_to(mean, shift.shape)
    z = (near[...] - mean) * root[0:1, :]
    near[...] = z
    gram[...] = add_diagonal(dot3(z, z, ((1,), (1,))), float(members - 1))
    set_inverse(inverse, gram, buf, low, scaled)


def solve_near(pieces, root, members):
    rows, cols = pieces[0].shape
    size = rows * len(pieces)
    square = jax.ShapeDtypeStruct((size, size), f32)
    return pl.pallas_call(
        functools.partial(near_kernel, members, len(pieces)),
        out_shape=(square, jax.ShapeDtypeStruct((size, cols), f32), jax.ShapeDtypeStruct((SUB, cols), f32)),
        in_specs=[VMEM] * (len(pieces) + 1),
        out_specs=(VMEM, VMEM, VMEM),
        scratch_shapes=solve_scratch(size),
        cost_estimate=pl.CostEstimate(flops=5_000_000_000, bytes_accessed=1, transcendentals=0),
        compiler_params=pltpu.CompilerParams(vmem_limit_bytes=VMEM_LIMIT),
        name="solve_near",
    )(*pieces, root)


def solve_scratch(size):
    return [
        pltpu.VMEM((size, size), f32),
        pltpu.VMEM((2 * SUB * (SUB + 1), size), f32),
        pltpu.VMEM((size, size), f32),
        pltpu.VMEM((size, size), f32),
    ]


def solve_kernel(places, *refs):
    count = len(places)
    pieces = refs[:count]
    inverse, near, shift, target, root, weights = refs[count : count + 6]
    fwd, gram, buf, low, scaled, second, far_z, right, out = refs[count + 6 :]
    rows = pieces[0].shape[0]
    own, size = target.shape[0], near.shape[0]
    members = 2 * size
    own_core, own_side = own_bits()

    def start(place):
        far, dy, dc = place
        core = own_core if dc == 0 else 1 - own_core
        side = own_side if dy == 0 else 1 - own_side
        return pl.multiple_of(far * own + (core * 2 + side) * rows, SUB)

    for piece, place in zip(pieces, places):
        if place[0] == 0:
            fwd[pl.ds(start(place), rows), :] = piece[...]
    scale = root[0:1, :]
    for i, piece in enumerate(pieces[count // 2 :]):
        far_z[i * rows : (i + 1) * rows, :] = (piece[...] - shift[0:1, :]) * scale
    residual = (target[...] - fwd[...]) * scale
    za, zb = near[...], far_z[...]
    side = dot3(zb, za, ((1,), (1,)))
    ca, cb = dot3(za, residual, ((1,), (1,))), dot3(zb, residual, ((1,), (1,)))
    mean = (jnp.sum(ca, axis=0, keepdims=True) + jnp.sum(cb, axis=0, keepdims=True)) / members
    ones = jnp.ones((size, own), f32)
    ra = jnp.concatenate([ca - mean, ones], axis=1)
    rb = jnp.concatenate([cb - mean, ones], axis=1)
    top = dot3(inverse[...], jnp.concatenate([side.T, ra], axis=1), ((1,), (0,)))
    drop = dot3(side, top, ((1,), (0,)))
    gram[...] = add_diagonal(dot3(zb, zb, ((1,), (1,))), float(members - 1)) - drop[:, :size]
    right[0:size, :] = top
    right[size:, size:] = rb - drop[:, size:]
    set_inverse(second, gram, buf, low, scaled)
    xb = dot3(second[...], right[size:, size:], ((1,), (0,)))
    xa = right[0:size, size:] - dot3(right[0:size, 0:size], xb, ((1,), (0,)))
    x = jnp.concatenate([xa, xb], axis=0)
    w, unit = x[:, :own], x[:, own:]
    w = w - unit * (jnp.sum(w, axis=0, keepdims=True) / jnp.sum(unit, axis=0, keepdims=True))
    w = w - jnp.mean(w, axis=0, keepdims=True)
    for i, place in enumerate(places):
        out[pl.ds(start(place), rows), :] = w[i * rows : (i + 1) * rows, :]
    weights[...] = out[...].T


def solve(pieces, places, inverse, near, shift, target, root):
    own, cols = target.shape
    size = near.shape[0]
    return pl.pallas_call(
        functools.partial(solve_kernel, places),
        out_shape=jax.ShapeDtypeStruct((own, 2 * size), f32),
        in_specs=[VMEM] * (len(pieces) + 5),
        out_specs=VMEM,
        scratch_shapes=[pltpu.VMEM((own, cols), f32)]
        + solve_scratch(size)
        + [
            pltpu.VMEM((size, size), f32),
            pltpu.VMEM((size, cols), f32),
            pltpu.VMEM((2 * size, size + 2 * own), f32),
            pltpu.VMEM((2 * size, own), f32),
        ],
        cost_estimate=pl.CostEstimate(flops=5_000_000_000, bytes_accessed=1, transcendentals=0),
        compiler_params=pltpu.CompilerParams(vmem_limit_bytes=VMEM_LIMIT),
        name="solve",
    )(*pieces, inverse, near, shift, target, root)


def update_kernel(weights, own_ens, *refs):
    parts = len(CUTS) - 1
    others, (out, buf, sems) = refs[:-3], refs[-3:]
    own, params = own_ens.shape
    width = params // PARTS
    copies = []
    for part in range(parts):
        for i in range(CUTS[part], CUTS[part + 1]):
            cols = slice(i * width, (i + 1) * width)
            at = slice((i - CUTS[part]) * width, (i - CUTS[part] + 1) * width)
            total = own_ens[:, cols]
            total = total + dot3(weights[:, :own], total, ((1,), (0,)))
            for far in range(1, len(others) // parts + 1):
                w = weights[:, far * own : (far + 1) * own]
                total = total + dot3(w, others[(far - 1) * parts + part][:, at], ((1,), (0,)))
            buf[:, cols] = total
            copies.append(pltpu.make_async_copy(buf.at[:, cols], out.at[:, cols], sems.at[i]))
            copies[-1].start()
    for copy in copies:
        copy.wait()


def update(weights, own_ens, others):
    own, params = own_ens.shape
    return pl.pallas_call(
        update_kernel,
        out_shape=jax.ShapeDtypeStruct((own, params), f32),
        in_specs=[VMEM] * (2 + len(others)),
        out_specs=HBM,
        scratch_shapes=[pltpu.VMEM((own, params), f32), pltpu.SemaphoreType.DMA((PARTS,))],
        cost_estimate=pl.CostEstimate(
            flops=2 * own * weights.shape[1] * params, bytes_accessed=4 * params * (own + weights.shape[1]), transcendentals=0
        ),
        compiler_params=pltpu.CompilerParams(vmem_limit_bytes=VMEM_LIMIT),
        name="update",
    )(weights, own_ens, *others)


def per_device(n_mem, n_par, operator, ensemble, noise, observations, variances, rows):
    index = lax.axis_index("par")
    side = lax.bitwise_and(lax.shift_right_logical(index, 1), 1)

    def swap(x, far, near):
        pairs = [
            (m * n_par + p, (m ^ far) * n_par + (p ^ near)) for m in range(n_mem) for p in range(n_par)
        ]
        return lax.ppermute(x, ("mem", "par"), pairs)

    width = ensemble.shape[1] // PARTS
    first, second, third = (ensemble[:, width * i : width * k] for i, k in zip(CUTS, CUTS[1:]))
    first = [swap(first, far, 0) for far in range(1, n_mem)]
    second = [swap(second, far, 0) for far in range(1, n_mem)]
    keep, send = forward(ensemble, operator)
    part = keep + swap(send, 0, 1)
    size = part.shape[0] // 2
    other = swap(lax.dynamic_slice_in_dim(part, (1 - side) * size, size, 0), 0, 2)
    other, first = lax.optimization_barrier((other, first))
    total = lax.dynamic_slice_in_dim(part, side * size, size, 0) + other
    target, root = lookup(rows, observations, variances, noise)
    stride = 4
    while stride < n_par:
        ways = min(4, n_par // stride)
        terms = [total] + [swap(total, 0, d * stride) for d in range(1, ways)]
        if stride == 4:
            terms, target, root, second = lax.optimization_barrier((terms, target, root, second))
        total = add_all(terms)
        stride *= ways
    places = [(far, dy, 0) for far in range(n_mem) for dy in range(2)]
    pieces = [total if (far, dy) == (0, 0) else swap(total, far, 2 * dy) for far, dy, _ in places]
    third, _ = lax.optimization_barrier((third, total))
    third = [swap(third, far, 0) for far in range(1, n_mem)]
    inverse, near, shift = solve_near(pieces, root, ensemble.shape[0] * n_mem)
    pieces += [swap(piece, 0, 1) for piece in pieces]
    places += [(far, dy, 1) for far, dy, _ in places]
    weights = solve(pieces, places, inverse, near, shift, target, root)
    return update(weights, ensemble, [part for far in zip(first, second, third) for part in far])


def solution(mesh):
    return jax.shard_map(
        functools.partial(per_device, mesh.shape["mem"], mesh.shape["par"]),
        mesh=mesh,
        in_specs=(P("par", None), P("mem", "par"), P("mem", None), P(), P(), P()),
        out_specs=P("mem", "par"),
        check_vma=False,
    )
```

```python
import functools

import jax
import jax.numpy as jnp
from jax import lax
from jax.experimental import pallas as pl
from jax.experimental.pallas import tpu as pltpu
from jax.sharding import PartitionSpec as P

f32 = jnp.float32
HIGHEST = lax.Precision.HIGHEST
SUB, LANE = 8, 128
BUF_ROWS = 2 * SUB * SUB + SUB
VMEM = pl.BlockSpec(memory_space=pltpu.VMEM)
HBM = pl.BlockSpec(memory_space=pltpu.HBM)
VMEM_LIMIT = 20 << 20
PARTS = 8
CUTS = (0, 1, 4, 5, 8)


def dot(a, b, dims, precision=HIGHEST):
    return lax.dot_general(a, b, (dims, ((), ())), precision=precision, preferred_element_type=f32)


def add_all(terms):
    terms = list(terms)
    while len(terms) > 1:
        pairs = [terms[i] + terms[i + 1] for i in range(0, len(terms) - 1, 2)]
        terms = pairs + ([terms[-1]] if len(terms) % 2 else [])
    return terms[0]


def pivot_rows(e, sets):
    n = len(e)
    e = [list(line) for line in e]
    sets = [list(rows) for rows in sets]
    low = [[None] * n for _ in range(n)]
    outs = [[None] * n for _ in sets]
    for a in range(0, n, 2):
        b = a + 1
        scale = 1.0 / (e[a][a] * e[b][b] - e[a][b] * e[a][b])
        aa, bb, ab = e[b][b] * scale, e[a][a] * scale, -(e[a][b] * scale)
        for rows, out in zip(sets, outs):
            out[a] = aa * rows[a] + ab * rows[b]
            out[b] = ab * rows[a] + bb * rows[b]
        for i in range(b + 1, n):
            la = e[a][i] * aa + e[b][i] * ab
            lb = e[a][i] * ab + e[b][i] * bb
            low[i][a], low[i][b] = la, lb
            for m in range(i, n):
                e[i][m] = e[i][m] - (la * e[a][m] + lb * e[b][m])
            for rows in sets:
                rows[i] = rows[i] - (la * rows[a] + lb * rows[b])
    for a in range(n - 4, -1, -2):
        for k in (a, a + 1):
            for out in outs:
                out[k] = out[k] - add_all(low[i][k] * out[i] for i in range(a + 2, n))
    return outs


def across(v, k):
    return jnp.broadcast_to(v[:, k : k + 1], v.shape)


def block_inverse(matrix, buf):
    size = matrix.shape[0]
    lane = lax.broadcasted_iota(jnp.int32, (SUB, size), 1)
    sub = lax.broadcasted_iota(jnp.int32, (SUB, size), 0)
    n = size // SUB
    square = SUB * SUB
    m = [matrix[SUB * i : SUB * (i + 1), :] for i in range(n)]
    low, scaled = [], []
    cols = [across(m[0], k) for k in range(SUB)]
    for j in range(n):
        at = SUB * j
        here = (lane >= at) & (lane < at + SUB)
        base = (j % 2) * BUF_ROWS

        def put(start, values):
            for k, value in enumerate(values):
                buf[base + start + SUB * k : base + start + SUB * (k + 1), :] = value

        def get(i):
            return jnp.broadcast_to(buf[base + i : base + i + 1, :], (SUB, size))

        put(0, cols)
        row = jnp.where(here, (lane - at == sub).astype(f32), m[j])
        put(2 * square, [row])
        e = [[get(SUB * k + i) if i <= k else None for k in range(SUB)] for i in range(SUB)]
        sets = [[get(2 * square + k) for k in range(SUB)]]
        if j + 1 < n:
            side = [across(m[j + 1], at + k) for k in range(SUB)]
            old = [across(m[j + 1], at + SUB + k) for k in range(SUB)]
            put(square, side)
            sets.append(side)
        outs = pivot_rows(e, sets)
        new = outs[0]
        if j + 1 < n:
            cols = [
                old[i] - add_all(get(square + SUB * k + i) * outs[1][k] for k in range(SUB)) for i in range(SUB)
            ]
            m[j + 1] = jnp.where(here, 0.0, m[j + 1]) - add_all(side[k] * new[k] for k in range(SUB))
        for i in range(j + 2, n):
            m[i] = jnp.where(here, 0.0, m[i]) - add_all(across(m[i], at + k) * new[k] for k in range(SUB))
        done = new[0]
        for i in range(1, SUB):
            done = jnp.where(sub == i, new[i], done)
        keep = lane < at + SUB
        low.append(jnp.where(keep, row, 0.0))
        scaled.append(jnp.where(keep, done, 0.0))
    return jnp.concatenate(low, axis=0), jnp.concatenate(scaled, axis=0)


def own_bits():
    index = lax.axis_index("par")
    return lax.bitwise_and(index, 1), lax.bitwise_and(lax.shift_right_logical(index, 1), 1)


def dot3(a, b, dims):
    parts = []
    for x in (a, b):
        high = x.astype(jnp.bfloat16)
        parts.append((high, (x - high.astype(f32)).astype(jnp.bfloat16)))
    (ah, al), (bh, bl) = parts
    mul = lambda x, y: lax.dot_general(x, y, (dims, ((), ())), preferred_element_type=f32)
    return mul(ah, bh) + (mul(ah, bl) + mul(al, bh))


def own_bits():
    index = lax.axis_index("par")
    return lax.bitwise_and(index, 1), lax.bitwise_and(lax.shift_right_logical(index, 1), 1)


def forward_kernel(steps, ens, op, keep, send, ens_buf, op_buf, acc, sems):
    depth = op.shape[0] // steps
    cut = lambda i: pl.ds(i * depth, depth)
    copies = [pltpu.make_async_copy(ens, ens_buf, sems.at[steps])]
    copies += [pltpu.make_async_copy(op.at[cut(i), :], op_buf.at[cut(i), :], sems.at[i]) for i in range(steps)]
    for copy in copies:
        copy.start()
    copies[0].wait()
    total = None
    for i in range(steps):
        copies[i + 1].wait()
        term = dot3(ens_buf[:, cut(i)], op_buf[cut(i), :], ((1,), (0,)))
        total = term if total is None else total + term
    acc[...] = total
    half = keep.shape[0]
    core, _ = own_bits()
    keep[...] = acc[pl.ds(pl.multiple_of(core * half, SUB), half), :]
    send[...] = acc[pl.ds(pl.multiple_of((1 - core) * half, SUB), half), :]


def forward(ens, op):
    members, params = ens.shape
    rows = op.shape[1]
    steps = 8 if params % (8 * LANE) == 0 else 1
    half = jax.ShapeDtypeStruct((members // 2, rows), f32)
    return pl.pallas_call(
        functools.partial(forward_kernel, steps),
        out_shape=(half, half),
        in_specs=[HBM, HBM],
        out_specs=(VMEM, VMEM),
        scratch_shapes=[
            pltpu.VMEM(ens.shape, f32),
            pltpu.VMEM(op.shape, f32),
            pltpu.VMEM((members, rows), f32),
            pltpu.SemaphoreType.DMA((steps + 1,)),
        ],
        cost_estimate=pl.CostEstimate(
            flops=2 * members * params * rows, bytes_accessed=4 * (members * params + params * rows), transcendentals=0
        ),
        compiler_params=pltpu.CompilerParams(vmem_limit_bytes=VMEM_LIMIT),
        name="forward",
    )(pltpu.with_memory_space_constraint(ens, pltpu.HBM), pltpu.with_memory_space_constraint(op, pltpu.HBM))


def lookup_kernel(rows, obs, var, noise, target, root):
    index = rows[...]
    high = lax.shift_right_logical(index, 7)
    low = lax.bitwise_and(index, LANE - 1)
    count = index.shape[1]
    blocks = obs.shape[0]
    pick_high = (lax.broadcasted_iota(jnp.int32, (blocks, count), 0) == high).astype(f32)
    pick_low = (lax.broadcasted_iota(jnp.int32, (LANE, count), 0) == low).astype(f32)
    obs_rows = jnp.sum(dot(obs[...], pick_high, ((0,), (0,))) * pick_low, axis=0, keepdims=True)
    var_rows = jnp.sum(dot(var[...], pick_high, ((0,), (0,))) * pick_low, axis=0, keepdims=True)
    target[...] = obs_rows + jnp.sqrt(var_rows) * noise[...]
    root[...] = jnp.broadcast_to(lax.rsqrt(var_rows), root.shape)


def lookup(rows, obs, var, noise):
    count = rows.shape[0]
    return pl.pallas_call(
        lookup_kernel,
        out_shape=(
            jax.ShapeDtypeStruct(noise.shape, f32),
            jax.ShapeDtypeStruct((SUB, count), f32),
        ),
        in_specs=[VMEM] * 4,
        out_specs=(VMEM, VMEM),
        cost_estimate=pl.CostEstimate(flops=2 * obs.shape[0] * LANE * count * 12, bytes_accessed=1 << 20, transcendentals=0),
        compiler_params=pltpu.CompilerParams(vmem_limit_bytes=VMEM_LIMIT),
        name="lookup",
    )(rows.reshape(1, count), obs.reshape(-1, LANE), var.reshape(-1, LANE), noise)


def fenced(body):
    pl.when(lax.axis_index("par") >= 0)(body)


def set_inverse(out, matrix, buf, low, scaled):
    @fenced
    def _():
        low[...], scaled[...] = block_inverse(matrix[...], buf)

    out[...] = dot3(low[...], scaled[...], ((0,), (0,)))


def add_diagonal(matrix, value):
    row = lax.broadcasted_iota(jnp.int32, matrix.shape, 0)
    col = lax.broadcasted_iota(jnp.int32, matrix.shape, 1)
    return matrix + jnp.where(row == col, value, 0.0)


def near_kernel(members, count, *refs):
    pieces = refs[:count]
    root, inverse, near, shift, gram, buf, low, scaled = refs[count:]
    rows = pieces[0].shape[0]
    for i, piece in enumerate(pieces):
        near[i * rows : (i + 1) * rows, :] = piece[...]
    mean = jnp.mean(near[...], axis=0, keepdims=True)
    shift[...] = jnp.broadcast_to(mean, shift.shape)
    z = (near[...] - mean) * root[0:1, :]
    near[...] = z
    gram[...] = add_diagonal(dot3(z, z, ((1,), (1,))), float(members - 1))
    set_inverse(inverse, gram, buf, low, scaled)


def solve_near(pieces, root, members):
    rows, cols = pieces[0].shape
    size = rows * len(pieces)
    square = jax.ShapeDtypeStruct((size, size), f32)
    return pl.pallas_call(
        functools.partial(near_kernel, members, len(pieces)),
        out_shape=(square, jax.ShapeDtypeStruct((size, cols), f32), jax.ShapeDtypeStruct((SUB, cols), f32)),
        in_specs=[VMEM] * (len(pieces) + 1),
        out_specs=(VMEM, VMEM, VMEM),
        scratch_shapes=solve_scratch(size),
        cost_estimate=pl.CostEstimate(flops=5_000_000_000, bytes_accessed=1, transcendentals=0),
        compiler_params=pltpu.CompilerParams(vmem_limit_bytes=VMEM_LIMIT),
        name="solve_near",
    )(*pieces, root)


def solve_scratch(size):
    return [
        pltpu.VMEM((size, size), f32),
        pltpu.VMEM((2 * BUF_ROWS, size), f32),
        pltpu.VMEM((size, size), f32),
        pltpu.VMEM((size, size), f32),
    ]


def solve_kernel(places, *refs):
    count = len(places)
    pieces = refs[:count]
    inverse, near, shift, target, root, weights = refs[count : count + 6]
    fwd, gram, buf, low, scaled, second, far_z, right, out = refs[count + 6 :]
    rows = pieces[0].shape[0]
    own, size = target.shape[0], near.shape[0]
    members = 2 * size
    own_core, own_side = own_bits()

    def start(place):
        far, dy, dc = place
        core = own_core if dc == 0 else 1 - own_core
        side = own_side if dy == 0 else 1 - own_side
        return pl.multiple_of(far * own + (core * 2 + side) * rows, SUB)

    for piece, place in zip(pieces, places):
        if place[0] == 0:
            fwd[pl.ds(start(place), rows), :] = piece[...]
    scale = root[0:1, :]
    for i, piece in enumerate(pieces[count // 2 :]):
        far_z[i * rows : (i + 1) * rows, :] = (piece[...] - shift[0:1, :]) * scale
    residual = (target[...] - fwd[...]) * scale
    za, zb = near[...], far_z[...]
    side = dot3(zb, za, ((1,), (1,)))
    ca, cb = dot3(za, residual, ((1,), (1,))), dot3(zb, residual, ((1,), (1,)))
    mean = (jnp.sum(ca, axis=0, keepdims=True) + jnp.sum(cb, axis=0, keepdims=True)) / members
    ones = jnp.ones((size, own), f32)
    ra = jnp.concatenate([ca - mean, ones], axis=1)
    rb = jnp.concatenate([cb - mean, ones], axis=1)
    top = dot3(inverse[...], jnp.concatenate([side.T, ra], axis=1), ((1,), (0,)))
    drop = dot3(side, top, ((1,), (0,)))
    gram[...] = add_diagonal(dot3(zb, zb, ((1,), (1,))), float(members - 1)) - drop[:, :size]
    right[0:size, :] = top
    right[size:, size:] = rb - drop[:, size:]
    set_inverse(second, gram, buf, low, scaled)
    xb = dot3(second[...], right[size:, size:], ((1,), (0,)))
    xa = right[0:size, size:] - dot3(right[0:size, 0:size], xb, ((1,), (0,)))
    x = jnp.concatenate([xa, xb], axis=0)
    w, unit = x[:, :own], x[:, own:]
    w = w - unit * (jnp.sum(w, axis=0, keepdims=True) / jnp.sum(unit, axis=0, keepdims=True))
    w = w - jnp.mean(w, axis=0, keepdims=True)
    for i, place in enumerate(places):
        out[pl.ds(start(place), rows), :] = w[i * rows : (i + 1) * rows, :]
    weights[...] = out[...].T


def solve(pieces, places, inverse, near, shift, target, root):
    own, cols = target.shape
    size = near.shape[0]
    return pl.pallas_call(
        functools.partial(solve_kernel, places),
        out_shape=jax.ShapeDtypeStruct((own, 2 * size), f32),
        in_specs=[VMEM] * (len(pieces) + 5),
        out_specs=VMEM,
        scratch_shapes=[pltpu.VMEM((own, cols), f32)]
        + solve_scratch(size)
        + [
            pltpu.VMEM((size, size), f32),
            pltpu.VMEM((size, cols), f32),
            pltpu.VMEM((2 * size, size + 2 * own), f32),
            pltpu.VMEM((2 * size, own), f32),
        ],
        cost_estimate=pl.CostEstimate(flops=5_000_000_000, bytes_accessed=1, transcendentals=0),
        compiler_params=pltpu.CompilerParams(vmem_limit_bytes=VMEM_LIMIT),
        name="solve",
    )(*pieces, inverse, near, shift, target, root)


def update_kernel(weights, own_ens, *refs):
    parts = len(CUTS) - 1
    others, (out, buf, sems) = refs[:-3], refs[-3:]
    own, params = own_ens.shape
    width = params // PARTS
    copies = []
    for part in range(parts):
        for i in range(CUTS[part], CUTS[part + 1]):
            cols = slice(i * width, (i + 1) * width)
            at = slice((i - CUTS[part]) * width, (i - CUTS[part] + 1) * width)
            total = own_ens[:, cols]
            total = total + dot3(weights[:, :own], total, ((1,), (0,)))
            for far in range(1, len(others) // parts + 1):
                w = weights[:, far * own : (far + 1) * own]
                total = total + dot3(w, others[(far - 1) * parts + part][:, at], ((1,), (0,)))
            buf[:, cols] = total
            copies.append(pltpu.make_async_copy(buf.at[:, cols], out.at[:, cols], sems.at[i]))
            copies[-1].start()
    for copy in copies:
        copy.wait()


def update(weights, own_ens, others):
    own, params = own_ens.shape
    return pl.pallas_call(
        update_kernel,
        out_shape=jax.ShapeDtypeStruct((own, params), f32),
        in_specs=[VMEM] * (2 + len(others)),
        out_specs=HBM,
        scratch_shapes=[pltpu.VMEM((own, params), f32), pltpu.SemaphoreType.DMA((PARTS,))],
        cost_estimate=pl.CostEstimate(
            flops=2 * own * weights.shape[1] * params, bytes_accessed=4 * params * (own + weights.shape[1]), transcendentals=0
        ),
        compiler_params=pltpu.CompilerParams(vmem_limit_bytes=VMEM_LIMIT),
        name="update",
    )(weights, own_ens, *others)


def per_device(n_mem, n_par, operator, ensemble, noise, observations, variances, rows):
    index = lax.axis_index("par")
    side = lax.bitwise_and(lax.shift_right_logical(index, 1), 1)

    def swap(x, far, near):
        pairs = [
            (m * n_par + p, (m ^ far) * n_par + (p ^ near)) for m in range(n_mem) for p in range(n_par)
        ]
        return lax.ppermute(x, ("mem", "par"), pairs)

    width = ensemble.shape[1] // PARTS
    first, second, third, last = (ensemble[:, width * i : width * k] for i, k in zip(CUTS, CUTS[1:]))
    first = [swap(first, far, 0) for far in range(1, n_mem)]
    second = [swap(second, far, 0) for far in range(1, n_mem)]
    keep, send = forward(ensemble, operator)
    part = keep + swap(send, 0, 1)
    size = part.shape[0] // 2
    other = swap(lax.dynamic_slice_in_dim(part, (1 - side) * size, size, 0), 0, 2)
    other, first = lax.optimization_barrier((other, first))
    total = lax.dynamic_slice_in_dim(part, side * size, size, 0) + other
    target, root = lookup(rows, observations, variances, noise)
    stride = 4
    while stride < n_par:
        ways = min(4, n_par // stride)
        terms = [total] + [swap(total, 0, d * stride) for d in range(1, ways)]
        if stride == 4:
            third, total = lax.optimization_barrier((third, total))
            third = [swap(third, far, 0) for far in range(1, n_mem)]
            terms, target, root, second = lax.optimization_barrier((terms, target, root, second))
        total = add_all(terms)
        stride *= ways
    places = [(far, dy, 0) for far in range(n_mem) for dy in range(2)]
    pieces = [total if (far, dy) == (0, 0) else swap(total, far, 2 * dy) for far, dy, _ in places]
    last, _ = lax.optimization_barrier((last, total))
    last = [swap(last, far, 0) for far in range(1, n_mem)]
    inverse, near, shift = solve_near(pieces, root, ensemble.shape[0] * n_mem)
    held, pieces[1], third = lax.optimization_barrier((pieces[0], pieces[1], third))
    pieces += [swap(piece, 0, 1) for piece in [held] + pieces[1:]]
    places += [(far, dy, 1) for far, dy, _ in places]
    weights = solve(pieces, places, inverse, near, shift, target, root)
    return update(weights, ensemble, [part for far in zip(first, second, third, last) for part in far])


def solution(mesh):
    return jax.shard_map(
        functools.partial(per_device, mesh.shape["mem"], mesh.shape["par"]),
        mesh=mesh,
        in_specs=(P("par", None), P("mem", "par"), P("mem", None), P(), P(), P()),
        out_specs=P("mem", "par"),
        check_vma=False,
    )
```

```python
import functools

import jax
import jax.numpy as jnp
from jax import lax
from jax.experimental import pallas as pl
from jax.experimental.pallas import tpu as pltpu
from jax.sharding import PartitionSpec as P

f32 = jnp.float32
HIGHEST = lax.Precision.HIGHEST
SUB, LANE = 8, 128
BUF_ROWS = 2 * SUB * SUB + SUB
VMEM = pl.BlockSpec(memory_space=pltpu.VMEM)
HBM = pl.BlockSpec(memory_space=pltpu.HBM)
VMEM_LIMIT = 20 << 20
PARTS = 8
CUTS = (0, 1, 4, 5, 8)


def dot(a, b, dims, precision=HIGHEST):
    return lax.dot_general(a, b, (dims, ((), ())), precision=precision, preferred_element_type=f32)


def add_all(terms):
    terms = list(terms)
    while len(terms) > 1:
        pairs = [terms[i] + terms[i + 1] for i in range(0, len(terms) - 1, 2)]
        terms = pairs + ([terms[-1]] if len(terms) % 2 else [])
    return terms[0]


def pivot_rows(e, sets):
    n = len(e)
    e = [list(line) for line in e]
    sets = [list(rows) for rows in sets]
    low = [[None] * n for _ in range(n)]
    outs = [[None] * n for _ in sets]
    for a in range(0, n, 2):
        b = a + 1
        scale = 1.0 / (e[a][a] * e[b][b] - e[a][b] * e[a][b])
        aa, bb, ab = e[b][b] * scale, e[a][a] * scale, -(e[a][b] * scale)
        for rows, out in zip(sets, outs):
            out[a] = aa * rows[a] + ab * rows[b]
            out[b] = ab * rows[a] + bb * rows[b]
        for i in range(b + 1, n):
            la = e[a][i] * aa + e[b][i] * ab
            lb = e[a][i] * ab + e[b][i] * bb
            low[i][a], low[i][b] = la, lb
            for m in range(i, n):
                e[i][m] = e[i][m] - (la * e[a][m] + lb * e[b][m])
            for rows in sets:
                rows[i] = rows[i] - (la * rows[a] + lb * rows[b])
    for a in range(n - 4, -1, -2):
        for k in (a, a + 1):
            for out in outs:
                out[k] = out[k] - add_all(low[i][k] * out[i] for i in range(a + 2, n))
    return outs


def across(v, k):
    return jnp.broadcast_to(v[:, k : k + 1], v.shape)


def block_inverse(matrix, buf):
    size = matrix.shape[0]
    lane = lax.broadcasted_iota(jnp.int32, (SUB, size), 1)
    sub = lax.broadcasted_iota(jnp.int32, (SUB, size), 0)
    n = size // SUB
    square = SUB * SUB
    m = [matrix[SUB * i : SUB * (i + 1), :] for i in range(n)]
    low, scaled = [], []
    cols = [across(m[0], k) for k in range(SUB)]
    for j in range(n):
        at = SUB * j
        here = (lane >= at) & (lane < at + SUB)
        base = (j % 2) * BUF_ROWS

        def put(start, values):
            for k, value in enumerate(values):
                buf[base + start + SUB * k : base + start + SUB * (k + 1), :] = value

        def get(i):
            return jnp.broadcast_to(buf[base + i : base + i + 1, :], (SUB, size))

        put(0, cols)
        row = jnp.where(here, (lane - at == sub).astype(f32), m[j])
        put(2 * square, [row])
        e = [[get(SUB * k + i) if i <= k else None for k in range(SUB)] for i in range(SUB)]
        sets = [[get(2 * square + k) for k in range(SUB)]]
        if j + 1 < n:
            side = [across(m[j + 1], at + k) for k in range(SUB)]
            old = [across(m[j + 1], at + SUB + k) for k in range(SUB)]
            put(square, side)
            sets.append(side)
        outs = pivot_rows(e, sets)
        new = outs[0]
        if j + 1 < n:
            cols = [
                old[i] - add_all(get(square + SUB * k + i) * outs[1][k] for k in range(SUB)) for i in range(SUB)
            ]
            m[j + 1] = jnp.where(here, 0.0, m[j + 1]) - add_all(side[k] * new[k] for k in range(SUB))
        for i in range(j + 2, n):
            m[i] = jnp.where(here, 0.0, m[i]) - add_all(across(m[i], at + k) * new[k] for k in range(SUB))
        done = new[0]
        for i in range(1, SUB):
            done = jnp.where(sub == i, new[i], done)
        keep = lane < at + SUB
        low.append(jnp.where(keep, row, 0.0))
        scaled.append(jnp.where(keep, done, 0.0))
    return jnp.concatenate(low, axis=0), jnp.concatenate(scaled, axis=0)


def own_bits():
    index = lax.axis_index("par")
    return lax.bitwise_and(index, 1), lax.bitwise_and(lax.shift_right_logical(index, 1), 1)


def halves(x):
    high = x.astype(jnp.bfloat16)
    return high, (x - high.astype(f32)).astype(jnp.bfloat16)


def matmul(a, b, dims=((1,), (0,))):
    return lax.dot_general(a, b, (dims, ((), ())), preferred_element_type=f32)


def dot3(a, b, dims):
    (ah, al), (bh, bl) = halves(a), halves(b)
    return matmul(ah, bh, dims) + (matmul(ah, bl, dims) + matmul(al, bh, dims))


def own_bits():
    index = lax.axis_index("par")
    return lax.bitwise_and(index, 1), lax.bitwise_and(lax.shift_right_logical(index, 1), 1)


def dot3(a, b, dims):
    parts = []
    for x in (a, b):
        high = x.astype(jnp.bfloat16)
        parts.append((high, (x - high.astype(f32)).astype(jnp.bfloat16)))
    (ah, al), (bh, bl) = parts
    mul = lambda x, y: lax.dot_general(x, y, (dims, ((), ())), preferred_element_type=f32)
    return mul(ah, bh) + (mul(ah, bl) + mul(al, bh))


def own_bits():
    index = lax.axis_index("par")
    return lax.bitwise_and(index, 1), lax.bitwise_and(lax.shift_right_logical(index, 1), 1)


def forward_kernel(steps, ens, op, keep, send, ens_buf, op_buf, acc, sems):
    depth = op.shape[0] // steps
    cut = lambda i: pl.ds(i * depth, depth)
    copies = [pltpu.make_async_copy(ens, ens_buf, sems.at[steps])]
    copies += [pltpu.make_async_copy(op.at[cut(i), :], op_buf.at[cut(i), :], sems.at[i]) for i in range(steps)]
    for copy in copies:
        copy.start()
    copies[0].wait()
    total = None
    for i in range(steps):
        copies[i + 1].wait()
        term = dot3(ens_buf[:, cut(i)], op_buf[cut(i), :], ((1,), (0,)))
        total = term if total is None else total + term
    acc[...] = total
    half = keep.shape[0]
    core, _ = own_bits()
    keep[...] = acc[pl.ds(pl.multiple_of(core * half, SUB), half), :]
    send[...] = acc[pl.ds(pl.multiple_of((1 - core) * half, SUB), half), :]


def forward(ens, op):
    members, params = ens.shape
    rows = op.shape[1]
    steps = 8 if params % (8 * LANE) == 0 else 1
    half = jax.ShapeDtypeStruct((members // 2, rows), f32)
    return pl.pallas_call(
        functools.partial(forward_kernel, steps),
        out_shape=(half, half),
        in_specs=[HBM, HBM],
        out_specs=(VMEM, VMEM),
        scratch_shapes=[
            pltpu.VMEM(ens.shape, f32),
            pltpu.VMEM(op.shape, f32),
            pltpu.VMEM((members, rows), f32),
            pltpu.SemaphoreType.DMA((steps + 1,)),
        ],
        cost_estimate=pl.CostEstimate(
            flops=2 * members * params * rows, bytes_accessed=4 * (members * params + params * rows), transcendentals=0
        ),
        compiler_params=pltpu.CompilerParams(vmem_limit_bytes=VMEM_LIMIT),
        name="forward",
    )(pltpu.with_memory_space_constraint(ens, pltpu.HBM), pltpu.with_memory_space_constraint(op, pltpu.HBM))


def lookup_kernel(rows, obs, var, noise, target, root):
    index = rows[...]
    high = lax.shift_right_logical(index, 7)
    low = lax.bitwise_and(index, LANE - 1)
    count = index.shape[1]
    blocks = obs.shape[0]
    pick_high = (lax.broadcasted_iota(jnp.int32, (blocks, count), 0) == high).astype(f32)
    pick_low = (lax.broadcasted_iota(jnp.int32, (LANE, count), 0) == low).astype(f32)
    obs_rows = jnp.sum(dot(obs[...], pick_high, ((0,), (0,))) * pick_low, axis=0, keepdims=True)
    var_rows = jnp.sum(dot(var[...], pick_high, ((0,), (0,))) * pick_low, axis=0, keepdims=True)
    target[...] = obs_rows + jnp.sqrt(var_rows) * noise[...]
    root[...] = jnp.broadcast_to(lax.rsqrt(var_rows), root.shape)


def lookup(rows, obs, var, noise):
    count = rows.shape[0]
    return pl.pallas_call(
        lookup_kernel,
        out_shape=(
            jax.ShapeDtypeStruct(noise.shape, f32),
            jax.ShapeDtypeStruct((SUB, count), f32),
        ),
        in_specs=[VMEM] * 4,
        out_specs=(VMEM, VMEM),
        cost_estimate=pl.CostEstimate(flops=2 * obs.shape[0] * LANE * count * 12, bytes_accessed=1 << 20, transcendentals=0),
        compiler_params=pltpu.CompilerParams(vmem_limit_bytes=VMEM_LIMIT),
        name="lookup",
    )(rows.reshape(1, count), obs.reshape(-1, LANE), var.reshape(-1, LANE), noise)


def fenced(body):
    pl.when(lax.axis_index("par") >= 0)(body)


def set_inverse(out, matrix, buf, low, scaled):
    @fenced
    def _():
        low[...], scaled[...] = block_inverse(matrix[...], buf)

    out[...] = dot3(low[...], scaled[...], ((0,), (0,)))


def add_diagonal(matrix, value):
    row = lax.broadcasted_iota(jnp.int32, matrix.shape, 0)
    col = lax.broadcasted_iota(jnp.int32, matrix.shape, 1)
    return matrix + jnp.where(row == col, value, 0.0)


def near_kernel(members, count, *refs):
    pieces = refs[:count]
    root, inverse, near, shift, gram, buf, low, scaled = refs[count:]
    rows = pieces[0].shape[0]
    for i, piece in enumerate(pieces):
        near[i * rows : (i + 1) * rows, :] = piece[...]
    mean = jnp.mean(near[...], axis=0, keepdims=True)
    shift[...] = jnp.broadcast_to(mean, shift.shape)
    z = (near[...] - mean) * root[0:1, :]
    near[...] = z
    gram[...] = add_diagonal(dot3(z, z, ((1,), (1,))), float(members - 1))
    set_inverse(inverse, gram, buf, low, scaled)


def solve_near(pieces, root, members):
    rows, cols = pieces[0].shape
    size = rows * len(pieces)
    square = jax.ShapeDtypeStruct((size, size), f32)
    return pl.pallas_call(
        functools.partial(near_kernel, members, len(pieces)),
        out_shape=(square, jax.ShapeDtypeStruct((size, cols), f32), jax.ShapeDtypeStruct((SUB, cols), f32)),
        in_specs=[VMEM] * (len(pieces) + 1),
        out_specs=(VMEM, VMEM, VMEM),
        scratch_shapes=solve_scratch(size),
        cost_estimate=pl.CostEstimate(flops=5_000_000_000, bytes_accessed=1, transcendentals=0),
        compiler_params=pltpu.CompilerParams(vmem_limit_bytes=VMEM_LIMIT),
        name="solve_near",
    )(*pieces, root)


def solve_scratch(size):
    return [
        pltpu.VMEM((size, size), f32),
        pltpu.VMEM((2 * BUF_ROWS, size), f32),
        pltpu.VMEM((size, size), f32),
        pltpu.VMEM((size, size), f32),
    ]


def solve_kernel(places, *refs):
    count = len(places)
    pieces = refs[:count]
    inverse, near, shift, target, root, weights = refs[count : count + 6]
    fwd, gram, buf, low, scaled, second, far_z, right, out = refs[count + 6 :]
    rows = pieces[0].shape[0]
    own, size = target.shape[0], near.shape[0]
    members = 2 * size
    own_core, own_side = own_bits()

    def start(place):
        far, dy, dc = place
        core = own_core if dc == 0 else 1 - own_core
        side = own_side if dy == 0 else 1 - own_side
        return pl.multiple_of(far * own + (core * 2 + side) * rows, SUB)

    for piece, place in zip(pieces, places):
        if place[0] == 0:
            fwd[pl.ds(start(place), rows), :] = piece[...]
    scale = root[0:1, :]
    for i, piece in enumerate(pieces[count // 2 :]):
        far_z[i * rows : (i + 1) * rows, :] = (piece[...] - shift[0:1, :]) * scale
    residual = (target[...] - fwd[...]) * scale
    za, zb = near[...], far_z[...]
    side = dot3(zb, za, ((1,), (1,)))
    ca, cb = dot3(za, residual, ((1,), (1,))), dot3(zb, residual, ((1,), (1,)))
    mean = (jnp.sum(ca, axis=0, keepdims=True) + jnp.sum(cb, axis=0, keepdims=True)) / members
    ones = jnp.ones((size, own), f32)
    ra = jnp.concatenate([ca - mean, ones], axis=1)
    rb = jnp.concatenate([cb - mean, ones], axis=1)
    top = dot3(inverse[...], jnp.concatenate([side.T, ra], axis=1), ((1,), (0,)))
    drop = dot3(side, top, ((1,), (0,)))
    gram[...] = add_diagonal(dot3(zb, zb, ((1,), (1,))), float(members - 1)) - drop[:, :size]
    right[0:size, :] = top
    right[size:, size:] = rb - drop[:, size:]
    set_inverse(second, gram, buf, low, scaled)
    xb = dot3(second[...], right[size:, size:], ((1,), (0,)))
    xa = right[0:size, size:] - dot3(right[0:size, 0:size], xb, ((1,), (0,)))
    x = jnp.concatenate([xa, xb], axis=0)
    w, unit = x[:, :own], x[:, own:]
    w = w - unit * (jnp.sum(w, axis=0, keepdims=True) / jnp.sum(unit, axis=0, keepdims=True))
    w = w - jnp.mean(w, axis=0, keepdims=True)
    for i, place in enumerate(places):
        out[pl.ds(start(place), rows), :] = w[i * rows : (i + 1) * rows, :]
    weights[...] = out[...].T


def solve(pieces, places, inverse, near, shift, target, root):
    own, cols = target.shape
    size = near.shape[0]
    return pl.pallas_call(
        functools.partial(solve_kernel, places),
        out_shape=jax.ShapeDtypeStruct((own, 2 * size), f32),
        in_specs=[VMEM] * (len(pieces) + 5),
        out_specs=VMEM,
        scratch_shapes=[pltpu.VMEM((own, cols), f32)]
        + solve_scratch(size)
        + [
            pltpu.VMEM((size, size), f32),
            pltpu.VMEM((size, cols), f32),
            pltpu.VMEM((2 * size, size + 2 * own), f32),
            pltpu.VMEM((2 * size, own), f32),
        ],
        cost_estimate=pl.CostEstimate(flops=5_000_000_000, bytes_accessed=1, transcendentals=0),
        compiler_params=pltpu.CompilerParams(vmem_limit_bytes=VMEM_LIMIT),
        name="solve",
    )(*pieces, inverse, near, shift, target, root)


def update_kernel(weights, own_ens, *refs):
    parts = len(CUTS) - 1
    others, (out, buf, sems) = refs[:-3], refs[-3:]
    width = out.shape[1] // PARTS
    w_high, w_low = halves(weights[...])
    copies = []
    for part in range(parts):
        for i in range(CUTS[part], CUTS[part + 1]):
            cols = slice(i * width, (i + 1) * width)
            at = slice((i - CUTS[part]) * width, (i - CUTS[part] + 1) * width)
            held = [own_ens[:, cols]] + [ref[:, at] for ref in others[part::parts]]
            high, low = halves(jnp.concatenate(held, axis=0))
            change = matmul(w_high, high) + (matmul(w_high, low) + matmul(w_low, high))
            buf[:, cols] = held[0] + change
            copies.append(pltpu.make_async_copy(buf.at[:, cols], out.at[:, cols], sems.at[i]))
            copies[-1].start()
    for copy in copies:
        copy.wait()


def update(weights, own_ens, others):
    own, params = own_ens.shape
    return pl.pallas_call(
        update_kernel,
        out_shape=jax.ShapeDtypeStruct((own, params), f32),
        in_specs=[VMEM] * (2 + len(others)),
        out_specs=HBM,
        scratch_shapes=[pltpu.VMEM((own, params), f32), pltpu.SemaphoreType.DMA((PARTS,))],
        cost_estimate=pl.CostEstimate(
            flops=2 * own * weights.shape[1] * params, bytes_accessed=4 * params * (own + weights.shape[1]), transcendentals=0
        ),
        compiler_params=pltpu.CompilerParams(vmem_limit_bytes=VMEM_LIMIT),
        name="update",
    )(weights, own_ens, *others)


def per_device(n_mem, n_par, operator, ensemble, noise, observations, variances, rows):
    index = lax.axis_index("par")
    side = lax.bitwise_and(lax.shift_right_logical(index, 1), 1)

    def swap(x, far, near):
        pairs = [
            (m * n_par + p, (m ^ far) * n_par + (p ^ near)) for m in range(n_mem) for p in range(n_par)
        ]
        return lax.ppermute(x, ("mem", "par"), pairs)

    width = ensemble.shape[1] // PARTS
    first, second, third, last = (ensemble[:, width * i : width * k] for i, k in zip(CUTS, CUTS[1:]))
    first = [swap(first, far, 0) for far in range(1, n_mem)]
    second = [swap(second, far, 0) for far in range(1, n_mem)]
    keep, send = forward(ensemble, operator)
    part = keep + swap(send, 0, 1)
    size = part.shape[0] // 2
    other = swap(lax.dynamic_slice_in_dim(part, (1 - side) * size, size, 0), 0, 2)
    other, first = lax.optimization_barrier((other, first))
    total = lax.dynamic_slice_in_dim(part, side * size, size, 0) + other
    target, root = lookup(rows, observations, variances, noise)
    stride = 4
    while stride < n_par:
        ways = min(4, n_par // stride)
        terms = [total] + [swap(total, 0, d * stride) for d in range(1, ways)]
        if stride == 4:
            third, total = lax.optimization_barrier((third, total))
            third = [swap(third, far, 0) for far in range(1, n_mem)]
            terms, target, root, second = lax.optimization_barrier((terms, target, root, second))
        total = add_all(terms)
        stride *= ways
    places = [(far, dy, 0) for far in range(n_mem) for dy in range(2)]
    pieces = [total if (far, dy) == (0, 0) else swap(total, far, 2 * dy) for far, dy, _ in places]
    last, _ = lax.optimization_barrier((last, total))
    last = [swap(last, far, 0) for far in range(1, n_mem)]
    inverse, near, shift = solve_near(pieces, root, ensemble.shape[0] * n_mem)
    mine, pieces[1], third = lax.optimization_barrier((pieces[0], pieces[1], third))
    pieces += [swap(piece, 0, 1) for piece in [mine] + pieces[1:]]
    places += [(far, dy, 1) for far, dy, _ in places]
    weights = solve(pieces, places, inverse, near, shift, target, root)
    return update(weights, ensemble, [part for far in zip(first, second, third, last) for part in far])


def solution(mesh):
    return jax.shard_map(
        functools.partial(per_device, mesh.shape["mem"], mesh.shape["par"]),
        mesh=mesh,
        in_specs=(P("par", None), P("mem", "par"), P("mem", None), P(), P(), P()),
        out_specs=P("mem", "par"),
        check_vma=False,
    )
```

```python
import functools

import jax
import jax.numpy as jnp
from jax import lax
from jax.experimental import pallas as pl
from jax.experimental.pallas import tpu as pltpu
from jax.sharding import PartitionSpec as P

f32 = jnp.float32
HIGHEST = lax.Precision.HIGHEST
SUB, LANE = 8, 128
BUF_ROWS = 2 * SUB * SUB + SUB
FAR_ROWS = 4
VMEM = pl.BlockSpec(memory_space=pltpu.VMEM)
HBM = pl.BlockSpec(memory_space=pltpu.HBM)
VMEM_LIMIT = 20 << 20
PARTS = 16
CUTS = (0, 1, 7, 9, 16)
STEP = 2


def dot(a, b, dims, precision=HIGHEST):
    return lax.dot_general(a, b, (dims, ((), ())), precision=precision, preferred_element_type=f32)


def add_all(terms):
    terms = list(terms)
    while len(terms) > 1:
        pairs = [terms[i] + terms[i + 1] for i in range(0, len(terms) - 1, 2)]
        terms = pairs + ([terms[-1]] if len(terms) % 2 else [])
    return terms[0]


def pivot_rows(e, sets):
    n = len(e)
    e = [list(line) for line in e]
    sets = [list(rows) for rows in sets]
    low = [[None] * n for _ in range(n)]
    outs = [[None] * n for _ in sets]
    for a in range(0, n, 2):
        b = a + 1
        scale = 1.0 / (e[a][a] * e[b][b] - e[a][b] * e[a][b])
        aa, bb, ab = e[b][b] * scale, e[a][a] * scale, -(e[a][b] * scale)
        for rows, out in zip(sets, outs):
            out[a] = aa * rows[a] + ab * rows[b]
            out[b] = ab * rows[a] + bb * rows[b]
        for i in range(b + 1, n):
            la = e[a][i] * aa + e[b][i] * ab
            lb = e[a][i] * ab + e[b][i] * bb
            low[i][a], low[i][b] = la, lb
            for m in range(i, n):
                e[i][m] = e[i][m] - (la * e[a][m] + lb * e[b][m])
            for rows in sets:
                rows[i] = rows[i] - (la * rows[a] + lb * rows[b])
    for a in range(n - 4, -1, -2):
        for k in (a, a + 1):
            for out in outs:
                out[k] = out[k] - add_all(low[i][k] * out[i] for i in range(a + 2, n))
    return outs


def across(v, k):
    return jnp.broadcast_to(v[:, k : k + 1], v.shape)


def block_inverse(matrix, buf):
    size = matrix.shape[0]
    lane = lax.broadcasted_iota(jnp.int32, (SUB, size), 1)
    sub = lax.broadcasted_iota(jnp.int32, (SUB, size), 0)
    n = size // SUB
    square = SUB * SUB
    m = [matrix[SUB * i : SUB * (i + 1), :] for i in range(n)]
    low, scaled = [], []
    cols = [across(m[0], k) for k in range(SUB)]
    for j in range(n):
        at = SUB * j
        here = (lane >= at) & (lane < at + SUB)
        base = (j % 2) * BUF_ROWS

        def put(start, values):
            for k, value in enumerate(values):
                buf[base + start + SUB * k : base + start + SUB * (k + 1), :] = value

        def get(i):
            return jnp.broadcast_to(buf[base + i : base + i + 1, :], (SUB, size))

        put(0, cols)
        row = jnp.where(here, (lane - at == sub).astype(f32), m[j])
        put(2 * square, [row])
        e = [[get(SUB * k + i) if i <= k else None for k in range(SUB)] for i in range(SUB)]
        sets = [[get(2 * square + k) for k in range(SUB)]]
        if j + 1 < n:
            side = [across(m[j + 1], at + k) for k in range(SUB)]
            old = [across(m[j + 1], at + SUB + k) for k in range(SUB)]
            put(square, side)
            sets.append(side)
        outs = pivot_rows(e, sets)
        new = outs[0]
        if j + 1 < n:
            cols = [
                old[i] - add_all(get(square + SUB * k + i) * outs[1][k] for k in range(SUB)) for i in range(SUB)
            ]
            m[j + 1] = jnp.where(here, 0.0, m[j + 1]) - add_all(side[k] * new[k] for k in range(SUB))
        done = new[0]
        for i in range(1, SUB):
            done = jnp.where(sub == i, new[i], done)
        far = j + 3 if n - j - 3 >= FAR_ROWS else n
        for i in range(j + 2, min(far, n)):
            m[i] = jnp.where(here, 0.0, m[i]) - add_all(across(m[i], at + k) * new[k] for k in range(SUB))
        if far < n:
            blank = lambda count: [jnp.zeros((count, size), f32)] if count else []
            rows = jnp.concatenate(blank(at) + [done] + blank(size - at - SUB), axis=0)
            drop = dot3(jnp.concatenate(m[far:], axis=0), rows, ((1,), (0,)))
            for i in range(far, n):
                m[i] = jnp.where(here, 0.0, m[i]) - drop[SUB * (i - far) : SUB * (i - far + 1), :]
        keep = lane < at + SUB
        low.append(jnp.where(keep, row, 0.0))
        scaled.append(jnp.where(keep, done, 0.0))
    return jnp.concatenate(low, axis=0), jnp.concatenate(scaled, axis=0)


def own_bits():
    index = lax.axis_index("par")
    return lax.bitwise_and(index, 1), lax.bitwise_and(lax.shift_right_logical(index, 1), 1)


def halves(x):
    high = x.astype(jnp.bfloat16)
    return high, (x - high.astype(f32)).astype(jnp.bfloat16)


def matmul(a, b, dims=((1,), (0,))):
    return lax.dot_general(a, b, (dims, ((), ())), preferred_element_type=f32)


def dot3(a, b, dims):
    (ah, al), (bh, bl) = halves(a), halves(b)
    return matmul(ah, bh, dims) + (matmul(ah, bl, dims) + matmul(al, bh, dims))


def own_bits():
    index = lax.axis_index("par")
    return lax.bitwise_and(index, 1), lax.bitwise_and(lax.shift_right_logical(index, 1), 1)


def dot3(a, b, dims):
    parts = []
    for x in (a, b):
        high = x.astype(jnp.bfloat16)
        parts.append((high, (x - high.astype(f32)).astype(jnp.bfloat16)))
    (ah, al), (bh, bl) = parts
    mul = lambda x, y: lax.dot_general(x, y, (dims, ((), ())), preferred_element_type=f32)
    return mul(ah, bh) + (mul(ah, bl) + mul(al, bh))


def own_bits():
    index = lax.axis_index("par")
    return lax.bitwise_and(index, 1), lax.bitwise_and(lax.shift_right_logical(index, 1), 1)


def forward_kernel(steps, ens, op, keep, send, ens_buf, op_buf, acc, sems):
    depth = op.shape[0] // steps
    cut = lambda i: pl.ds(i * depth, depth)
    copies = [pltpu.make_async_copy(ens, ens_buf, sems.at[steps])]
    copies += [pltpu.make_async_copy(op.at[cut(i), :], op_buf.at[cut(i), :], sems.at[i]) for i in range(steps)]
    for copy in copies:
        copy.start()
    copies[0].wait()
    total = None
    for i in range(steps):
        copies[i + 1].wait()
        term = dot3(ens_buf[:, cut(i)], op_buf[cut(i), :], ((1,), (0,)))
        total = term if total is None else total + term
    acc[...] = total
    half = keep.shape[0]
    core, _ = own_bits()
    keep[...] = acc[pl.ds(pl.multiple_of(core * half, SUB), half), :]
    send[...] = acc[pl.ds(pl.multiple_of((1 - core) * half, SUB), half), :]


def forward(ens, op):
    members, params = ens.shape
    rows = op.shape[1]
    steps = 8 if params % (8 * LANE) == 0 else 1
    half = jax.ShapeDtypeStruct((members // 2, rows), f32)
    return pl.pallas_call(
        functools.partial(forward_kernel, steps),
        out_shape=(half, half),
        in_specs=[HBM, HBM],
        out_specs=(VMEM, VMEM),
        scratch_shapes=[
            pltpu.VMEM(ens.shape, f32),
            pltpu.VMEM(op.shape, f32),
            pltpu.VMEM((members, rows), f32),
            pltpu.SemaphoreType.DMA((steps + 1,)),
        ],
        cost_estimate=pl.CostEstimate(
            flops=2 * members * params * rows, bytes_accessed=4 * (members * params + params * rows), transcendentals=0
        ),
        compiler_params=pltpu.CompilerParams(vmem_limit_bytes=VMEM_LIMIT),
        name="forward",
    )(pltpu.with_memory_space_constraint(ens, pltpu.HBM), pltpu.with_memory_space_constraint(op, pltpu.HBM))


def lookup_kernel(rows, obs, var, noise, target, root):
    index = rows[...]
    high = lax.shift_right_logical(index, 7)
    low = lax.bitwise_and(index, LANE - 1)
    count = index.shape[1]
    blocks = obs.shape[0]
    pick_high = (lax.broadcasted_iota(jnp.int32, (blocks, count), 0) == high).astype(f32)
    pick_low = (lax.broadcasted_iota(jnp.int32, (LANE, count), 0) == low).astype(f32)
    obs_rows = jnp.sum(dot(obs[...], pick_high, ((0,), (0,))) * pick_low, axis=0, keepdims=True)
    var_rows = jnp.sum(dot(var[...], pick_high, ((0,), (0,))) * pick_low, axis=0, keepdims=True)
    target[...] = obs_rows + jnp.sqrt(var_rows) * noise[...]
    root[...] = jnp.broadcast_to(lax.rsqrt(var_rows), root.shape)


def lookup(rows, obs, var, noise):
    count = rows.shape[0]
    return pl.pallas_call(
        lookup_kernel,
        out_shape=(
            jax.ShapeDtypeStruct(noise.shape, f32),
            jax.ShapeDtypeStruct((SUB, count), f32),
        ),
        in_specs=[VMEM] * 4,
        out_specs=(VMEM, VMEM),
        cost_estimate=pl.CostEstimate(flops=2 * obs.shape[0] * LANE * count * 12, bytes_accessed=1 << 20, transcendentals=0),
        compiler_params=pltpu.CompilerParams(vmem_limit_bytes=VMEM_LIMIT),
        name="lookup",
    )(rows.reshape(1, count), obs.reshape(-1, LANE), var.reshape(-1, LANE), noise)


def fenced(body):
    pl.when(lax.axis_index("par") >= 0)(body)


def set_inverse(out, matrix, buf, low, scaled):
    @fenced
    def _():
        low[...], scaled[...] = block_inverse(matrix[...], buf)

    out[...] = dot3(low[...], scaled[...], ((0,), (0,)))


def add_diagonal(matrix, value):
    row = lax.broadcasted_iota(jnp.int32, matrix.shape, 0)
    col = lax.broadcasted_iota(jnp.int32, matrix.shape, 1)
    return matrix + jnp.where(row == col, value, 0.0)


def near_kernel(members, count, *refs):
    pieces = refs[:count]
    root, inverse, near, shift, gram, buf, low, scaled = refs[count:]
    rows = pieces[0].shape[0]
    for i, piece in enumerate(pieces):
        near[i * rows : (i + 1) * rows, :] = piece[...]
    mean = jnp.mean(near[...], axis=0, keepdims=True)
    shift[...] = jnp.broadcast_to(mean, shift.shape)
    z = (near[...] - mean) * root[0:1, :]
    near[...] = z
    gram[...] = add_diagonal(dot3(z, z, ((1,), (1,))), float(members - 1))
    set_inverse(inverse, gram, buf, low, scaled)


def solve_near(pieces, root, members):
    rows, cols = pieces[0].shape
    size = rows * len(pieces)
    square = jax.ShapeDtypeStruct((size, size), f32)
    return pl.pallas_call(
        functools.partial(near_kernel, members, len(pieces)),
        out_shape=(square, jax.ShapeDtypeStruct((size, cols), f32), jax.ShapeDtypeStruct((SUB, cols), f32)),
        in_specs=[VMEM] * (len(pieces) + 1),
        out_specs=(VMEM, VMEM, VMEM),
        scratch_shapes=solve_scratch(size),
        cost_estimate=pl.CostEstimate(flops=5_000_000_000, bytes_accessed=1, transcendentals=0),
        compiler_params=pltpu.CompilerParams(vmem_limit_bytes=VMEM_LIMIT),
        name="solve_near",
    )(*pieces, root)


def solve_scratch(size):
    return [
        pltpu.VMEM((size, size), f32),
        pltpu.VMEM((2 * BUF_ROWS, size), f32),
        pltpu.VMEM((size, size), f32),
        pltpu.VMEM((size, size), f32),
    ]


def solve_kernel(places, *refs):
    count = len(places)
    pieces = refs[:count]
    inverse, near, shift, target, root, weights = refs[count : count + 6]
    fwd, gram, buf, low, scaled, second, far_z, right, out = refs[count + 6 :]
    rows = pieces[0].shape[0]
    own, size = target.shape[0], near.shape[0]
    members = 2 * size
    own_core, own_side = own_bits()

    def start(place):
        far, dy, dc = place
        core = own_core if dc == 0 else 1 - own_core
        side = own_side if dy == 0 else 1 - own_side
        return pl.multiple_of(far * own + (core * 2 + side) * rows, SUB)

    for piece, place in zip(pieces, places):
        if place[0] == 0:
            fwd[pl.ds(start(place), rows), :] = piece[...]
    scale = root[0:1, :]
    for i, piece in enumerate(pieces[count // 2 :]):
        far_z[i * rows : (i + 1) * rows, :] = (piece[...] - shift[0:1, :]) * scale
    residual = (target[...] - fwd[...]) * scale
    za, zb = near[...], far_z[...]
    side = dot3(zb, za, ((1,), (1,)))
    ca, cb = dot3(za, residual, ((1,), (1,))), dot3(zb, residual, ((1,), (1,)))
    mean = (jnp.sum(ca, axis=0, keepdims=True) + jnp.sum(cb, axis=0, keepdims=True)) / members
    ones = jnp.ones((size, own), f32)
    ra = jnp.concatenate([ca - mean, ones], axis=1)
    rb = jnp.concatenate([cb - mean, ones], axis=1)
    top = dot3(inverse[...], jnp.concatenate([side.T, ra], axis=1), ((1,), (0,)))
    drop = dot3(side, top, ((1,), (0,)))
    gram[...] = add_diagonal(dot3(zb, zb, ((1,), (1,))), float(members - 1)) - drop[:, :size]
    right[0:size, :] = top
    right[size:, size:] = rb - drop[:, size:]
    set_inverse(second, gram, buf, low, scaled)
    xb = dot3(second[...], right[size:, size:], ((1,), (0,)))
    xa = right[0:size, size:] - dot3(right[0:size, 0:size], xb, ((1,), (0,)))
    x = jnp.concatenate([xa, xb], axis=0)
    w, unit = x[:, :own], x[:, own:]
    w = w - unit * (jnp.sum(w, axis=0, keepdims=True) / jnp.sum(unit, axis=0, keepdims=True))
    w = w - jnp.mean(w, axis=0, keepdims=True)
    for i, place in enumerate(places):
        out[pl.ds(start(place), rows), :] = w[i * rows : (i + 1) * rows, :]
    weights[...] = out[...].T


def solve(pieces, places, inverse, near, shift, target, root):
    own, cols = target.shape
    size = near.shape[0]
    return pl.pallas_call(
        functools.partial(solve_kernel, places),
        out_shape=jax.ShapeDtypeStruct((own, 2 * size), f32),
        in_specs=[VMEM] * (len(pieces) + 5),
        out_specs=VMEM,
        scratch_shapes=[pltpu.VMEM((own, cols), f32)]
        + solve_scratch(size)
        + [
            pltpu.VMEM((size, size), f32),
            pltpu.VMEM((size, cols), f32),
            pltpu.VMEM((2 * size, size + 2 * own), f32),
            pltpu.VMEM((2 * size, own), f32),
        ],
        cost_estimate=pl.CostEstimate(flops=5_000_000_000, bytes_accessed=1, transcendentals=0),
        compiler_params=pltpu.CompilerParams(vmem_limit_bytes=VMEM_LIMIT),
        name="solve",
    )(*pieces, inverse, near, shift, target, root)


def update_kernel(weights, own_ens, *refs):
    parts = len(CUTS) - 1
    others, (out, buf, sems) = refs[:-3], refs[-3:]
    width = out.shape[1] // PARTS
    w_high, w_low = halves(weights[...])
    copies = []
    for part in range(parts):
        first, end = CUTS[part : part + 2]
        for i in range(first, end, STEP):
            last = min(i + STEP, end)
            cols = slice(i * width, last * width)
            at = slice((i - first) * width, (last - first) * width)
            held = [own_ens[:, cols]] + [ref[:, at] for ref in others[part::parts]]
            high, low = halves(jnp.concatenate(held, axis=0))
            change = matmul(w_high, high) + (matmul(w_high, low) + matmul(w_low, high))
            buf[:, cols] = held[0] + change
            copies.append(pltpu.make_async_copy(buf.at[:, cols], out.at[:, cols], sems.at[i]))
            copies[-1].start()
    for copy in copies:
        copy.wait()


def update(weights, own_ens, others):
    own, params = own_ens.shape
    return pl.pallas_call(
        update_kernel,
        out_shape=jax.ShapeDtypeStruct((own, params), f32),
        in_specs=[VMEM] * (2 + len(others)),
        out_specs=HBM,
        scratch_shapes=[pltpu.VMEM((own, params), f32), pltpu.SemaphoreType.DMA((PARTS,))],
        cost_estimate=pl.CostEstimate(
            flops=2 * own * weights.shape[1] * params, bytes_accessed=4 * params * (own + weights.shape[1]), transcendentals=0
        ),
        compiler_params=pltpu.CompilerParams(vmem_limit_bytes=VMEM_LIMIT),
        name="update",
    )(weights, own_ens, *others)


def per_device(n_mem, n_par, operator, ensemble, noise, observations, variances, rows):
    index = lax.axis_index("par")
    side = lax.bitwise_and(lax.shift_right_logical(index, 1), 1)

    def swap(x, far, near):
        pairs = [
            (m * n_par + p, (m ^ far) * n_par + (p ^ near)) for m in range(n_mem) for p in range(n_par)
        ]
        return lax.ppermute(x, ("mem", "par"), pairs)

    width = ensemble.shape[1] // PARTS
    first, second, third, last = (ensemble[:, width * i : width * k] for i, k in zip(CUTS, CUTS[1:]))
    first = [swap(first, far, 0) for far in range(1, n_mem)]
    second = [swap(second, far, 0) for far in range(1, n_mem)]
    keep, send = forward(ensemble, operator)
    part = keep + swap(send, 0, 1)
    size = part.shape[0] // 2
    other = swap(lax.dynamic_slice_in_dim(part, (1 - side) * size, size, 0), 0, 2)
    other, first = lax.optimization_barrier((other, first))
    total = lax.dynamic_slice_in_dim(part, side * size, size, 0) + other
    target, root = lookup(rows, observations, variances, noise)
    stride = 4
    while stride < n_par:
        ways = min(4, n_par // stride)
        terms = [total] + [swap(total, 0, d * stride) for d in range(1, ways)]
        if stride == 4:
            third, total = lax.optimization_barrier((third, total))
            third = [swap(third, far, 0) for far in range(1, n_mem)]
            terms, target, root, second = lax.optimization_barrier((terms, target, root, second))
        total = add_all(terms)
        stride *= ways
    places = [(far, dy, 0) for far in range(n_mem) for dy in range(2)]
    pieces = [total if (far, dy) == (0, 0) else swap(total, far, 2 * dy) for far, dy, _ in places]
    last, _ = lax.optimization_barrier((last, total))
    last = [swap(last, far, 0) for far in range(1, n_mem)]
    inverse, near, shift = solve_near(pieces, root, ensemble.shape[0] * n_mem)
    mine, pieces[1], third = lax.optimization_barrier((pieces[0], pieces[1], third))
    pieces += [swap(piece, 0, 1) for piece in [mine] + pieces[1:]]
    places += [(far, dy, 1) for far, dy, _ in places]
    weights = solve(pieces, places, inverse, near, shift, target, root)
    return update(weights, ensemble, [part for far in zip(first, second, third, last) for part in far])


def solution(mesh):
    return jax.shard_map(
        functools.partial(per_device, mesh.shape["mem"], mesh.shape["par"]),
        mesh=mesh,
        in_specs=(P("par", None), P("mem", "par"), P("mem", None), P(), P(), P()),
        out_specs=P("mem", "par"),
        check_vma=False,
    )
```

```python
import functools

import jax
import jax.numpy as jnp
from jax import lax
from jax.experimental import pallas as pl
from jax.experimental.pallas import tpu as pltpu
from jax.sharding import PartitionSpec as P

f32 = jnp.float32
HIGHEST = lax.Precision.HIGHEST
SUB, LANE = 8, 128
BUF_ROWS = 2 * SUB * SUB + SUB
FAR_ROWS = 4
VMEM = pl.BlockSpec(memory_space=pltpu.VMEM)
HBM = pl.BlockSpec(memory_space=pltpu.HBM)
VMEM_LIMIT = 20 << 20
PARTS = 16
CUTS = (0, 1, 6, 9, 16)
STEP = 2


def dot(a, b, dims, precision=HIGHEST):
    return lax.dot_general(a, b, (dims, ((), ())), precision=precision, preferred_element_type=f32)


def add_all(terms):
    terms = list(terms)
    while len(terms) > 1:
        pairs = [terms[i] + terms[i + 1] for i in range(0, len(terms) - 1, 2)]
        terms = pairs + ([terms[-1]] if len(terms) % 2 else [])
    return terms[0]


def pivot_rows(e, sets):
    n = len(e)
    e = [list(line) for line in e]
    sets = [list(rows) for rows in sets]
    low = [[None] * n for _ in range(n)]
    outs = [[None] * n for _ in sets]
    for a in range(0, n, 2):
        b = a + 1
        scale = 1.0 / (e[a][a] * e[b][b] - e[a][b] * e[a][b])
        aa, bb, ab = e[b][b] * scale, e[a][a] * scale, -(e[a][b] * scale)
        for rows, out in zip(sets, outs):
            out[a] = aa * rows[a] + ab * rows[b]
            out[b] = ab * rows[a] + bb * rows[b]
        for i in range(b + 1, n):
            la = e[a][i] * aa + e[b][i] * ab
            lb = e[a][i] * ab + e[b][i] * bb
            low[i][a], low[i][b] = la, lb
            for m in range(i, n):
                e[i][m] = e[i][m] - (la * e[a][m] + lb * e[b][m])
            for rows in sets:
                rows[i] = rows[i] - (la * rows[a] + lb * rows[b])
    for a in range(n - 4, -1, -2):
        for k in (a, a + 1):
            for out in outs:
                out[k] = out[k] - add_all(low[i][k] * out[i] for i in range(a + 2, n))
    return outs


def across(v, k):
    return jnp.broadcast_to(v[:, k : k + 1], v.shape)


def block_inverse(matrix, buf):
    size = matrix.shape[0]
    lane = lax.broadcasted_iota(jnp.int32, (SUB, size), 1)
    sub = lax.broadcasted_iota(jnp.int32, (SUB, size), 0)
    n = size // SUB
    square = SUB * SUB
    m = [matrix[SUB * i : SUB * (i + 1), :] for i in range(n)]
    low, scaled = [], []
    cols = [across(m[0], k) for k in range(SUB)]
    for j in range(n):
        at = SUB * j
        here = (lane >= at) & (lane < at + SUB)
        base = (j % 2) * BUF_ROWS

        def put(start, values):
            for k, value in enumerate(values):
                buf[base + start + SUB * k : base + start + SUB * (k + 1), :] = value

        def get(i):
            return jnp.broadcast_to(buf[base + i : base + i + 1, :], (SUB, size))

        put(0, cols)
        row = jnp.where(here, (lane - at == sub).astype(f32), m[j])
        put(2 * square, [row])
        e = [[get(SUB * k + i) if i <= k else None for k in range(SUB)] for i in range(SUB)]
        sets = [[get(2 * square + k) for k in range(SUB)]]
        if j + 1 < n:
            side = [across(m[j + 1], at + k) for k in range(SUB)]
            old = [across(m[j + 1], at + SUB + k) for k in range(SUB)]
            put(square, side)
            sets.append(side)
        outs = pivot_rows(e, sets)
        new = outs[0]
        if j + 1 < n:
            cols = [
                old[i] - add_all(get(square + SUB * k + i) * outs[1][k] for k in range(SUB)) for i in range(SUB)
            ]
            m[j + 1] = jnp.where(here, 0.0, m[j + 1]) - add_all(side[k] * new[k] for k in range(SUB))
        done = new[0]
        for i in range(1, SUB):
            done = jnp.where(sub == i, new[i], done)
        far = j + 3 if n - j - 3 >= FAR_ROWS else n
        for i in range(j + 2, min(far, n)):
            m[i] = jnp.where(here, 0.0, m[i]) - add_all(across(m[i], at + k) * new[k] for k in range(SUB))
        if far < n:
            blank = lambda count: [jnp.zeros((count, size), f32)] if count else []
            rows = jnp.concatenate(blank(at) + [done] + blank(size - at - SUB), axis=0)
            drop = dot3(jnp.concatenate(m[far:], axis=0), rows, ((1,), (0,)))
            for i in range(far, n):
                m[i] = jnp.where(here, 0.0, m[i]) - drop[SUB * (i - far) : SUB * (i - far + 1), :]
        keep = lane < at + SUB
        low.append(jnp.where(keep, row, 0.0))
        scaled.append(jnp.where(keep, done, 0.0))
    return jnp.concatenate(low, axis=0), jnp.concatenate(scaled, axis=0)


def own_bits():
    index = lax.axis_index("par")
    return lax.bitwise_and(index, 1), lax.bitwise_and(lax.shift_right_logical(index, 1), 1)


def halves(x):
    high = x.astype(jnp.bfloat16)
    return high, (x - high.astype(f32)).astype(jnp.bfloat16)


def matmul(a, b, dims=((1,), (0,))):
    return lax.dot_general(a, b, (dims, ((), ())), preferred_element_type=f32)


def dot3(a, b, dims):
    (ah, al), (bh, bl) = halves(a), halves(b)
    return matmul(ah, bh, dims) + (matmul(ah, bl, dims) + matmul(al, bh, dims))


def own_bits():
    index = lax.axis_index("par")
    return lax.bitwise_and(index, 1), lax.bitwise_and(lax.shift_right_logical(index, 1), 1)


def dot3(a, b, dims):
    parts = []
    for x in (a, b):
        high = x.astype(jnp.bfloat16)
        parts.append((high, (x - high.astype(f32)).astype(jnp.bfloat16)))
    (ah, al), (bh, bl) = parts
    mul = lambda x, y: lax.dot_general(x, y, (dims, ((), ())), preferred_element_type=f32)
    return mul(ah, bh) + (mul(ah, bl) + mul(al, bh))


def own_bits():
    index = lax.axis_index("par")
    return lax.bitwise_and(index, 1), lax.bitwise_and(lax.shift_right_logical(index, 1), 1)


def forward_kernel(steps, ens, op, keep, send, ens_buf, op_buf, acc, sems):
    depth = op.shape[0] // steps
    cut = lambda i: pl.ds(i * depth, depth)
    copies = [pltpu.make_async_copy(ens, ens_buf, sems.at[steps])]
    copies += [pltpu.make_async_copy(op.at[cut(i), :], op_buf.at[cut(i), :], sems.at[i]) for i in range(steps)]
    for copy in copies:
        copy.start()
    copies[0].wait()
    total = None
    for i in range(steps):
        copies[i + 1].wait()
        term = dot3(ens_buf[:, cut(i)], op_buf[cut(i), :], ((1,), (0,)))
        total = term if total is None else total + term
    acc[...] = total
    half = keep.shape[0]
    core, _ = own_bits()
    keep[...] = acc[pl.ds(pl.multiple_of(core * half, SUB), half), :]
    send[...] = acc[pl.ds(pl.multiple_of((1 - core) * half, SUB), half), :]


def forward(ens, op):
    members, params = ens.shape
    rows = op.shape[1]
    steps = 8 if params % (8 * LANE) == 0 else 1
    half = jax.ShapeDtypeStruct((members // 2, rows), f32)
    return pl.pallas_call(
        functools.partial(forward_kernel, steps),
        out_shape=(half, half),
        in_specs=[HBM, HBM],
        out_specs=(VMEM, VMEM),
        scratch_shapes=[
            pltpu.VMEM(ens.shape, f32),
            pltpu.VMEM(op.shape, f32),
            pltpu.VMEM((members, rows), f32),
            pltpu.SemaphoreType.DMA((steps + 1,)),
        ],
        cost_estimate=pl.CostEstimate(
            flops=2 * members * params * rows, bytes_accessed=4 * (members * params + params * rows), transcendentals=0
        ),
        compiler_params=pltpu.CompilerParams(vmem_limit_bytes=VMEM_LIMIT),
        name="forward",
    )(pltpu.with_memory_space_constraint(ens, pltpu.HBM), pltpu.with_memory_space_constraint(op, pltpu.HBM))


def lookup_kernel(rows, obs, var, noise, target, root):
    index = rows[...]
    high = lax.shift_right_logical(index, 7)
    low = lax.bitwise_and(index, LANE - 1)
    count = index.shape[1]
    blocks = obs.shape[0]
    pick_high = (lax.broadcasted_iota(jnp.int32, (blocks, count), 0) == high).astype(f32)
    pick_low = (lax.broadcasted_iota(jnp.int32, (LANE, count), 0) == low).astype(f32)
    obs_rows = jnp.sum(dot(obs[...], pick_high, ((0,), (0,))) * pick_low, axis=0, keepdims=True)
    var_rows = jnp.sum(dot(var[...], pick_high, ((0,), (0,))) * pick_low, axis=0, keepdims=True)
    target[...] = obs_rows + jnp.sqrt(var_rows) * noise[...]
    root[...] = jnp.broadcast_to(lax.rsqrt(var_rows), root.shape)


def lookup(rows, obs, var, noise):
    count = rows.shape[0]
    return pl.pallas_call(
        lookup_kernel,
        out_shape=(
            jax.ShapeDtypeStruct(noise.shape, f32),
            jax.ShapeDtypeStruct((SUB, count), f32),
        ),
        in_specs=[VMEM] * 4,
        out_specs=(VMEM, VMEM),
        cost_estimate=pl.CostEstimate(flops=2 * obs.shape[0] * LANE * count * 12, bytes_accessed=1 << 20, transcendentals=0),
        compiler_params=pltpu.CompilerParams(vmem_limit_bytes=VMEM_LIMIT),
        name="lookup",
    )(rows.reshape(1, count), obs.reshape(-1, LANE), var.reshape(-1, LANE), noise)


def fenced(body):
    pl.when(lax.axis_index("par") >= 0)(body)


def set_inverse(out, matrix, buf, low, scaled):
    @fenced
    def _():
        low[...], scaled[...] = block_inverse(matrix[...], buf)

    out[...] = dot3(low[...], scaled[...], ((0,), (0,)))


def add_diagonal(matrix, value):
    row = lax.broadcasted_iota(jnp.int32, matrix.shape, 0)
    col = lax.broadcasted_iota(jnp.int32, matrix.shape, 1)
    return matrix + jnp.where(row == col, value, 0.0)


def near_kernel(members, count, *refs):
    pieces = refs[:count]
    root, inverse, near, shift, gram, buf, low, scaled = refs[count:]
    rows = pieces[0].shape[0]
    for i, piece in enumerate(pieces):
        near[i * rows : (i + 1) * rows, :] = piece[...]
    mean = jnp.mean(near[...], axis=0, keepdims=True)
    shift[...] = jnp.broadcast_to(mean, shift.shape)
    z = (near[...] - mean) * root[0:1, :]
    near[...] = z
    gram[...] = add_diagonal(dot3(z, z, ((1,), (1,))), float(members - 1))
    set_inverse(inverse, gram, buf, low, scaled)


def solve_near(pieces, root, members):
    rows, cols = pieces[0].shape
    size = rows * len(pieces)
    square = jax.ShapeDtypeStruct((size, size), f32)
    return pl.pallas_call(
        functools.partial(near_kernel, members, len(pieces)),
        out_shape=(square, jax.ShapeDtypeStruct((size, cols), f32), jax.ShapeDtypeStruct((SUB, cols), f32)),
        in_specs=[VMEM] * (len(pieces) + 1),
        out_specs=(VMEM, VMEM, VMEM),
        scratch_shapes=solve_scratch(size),
        cost_estimate=pl.CostEstimate(flops=5_000_000_000, bytes_accessed=1, transcendentals=0),
        compiler_params=pltpu.CompilerParams(vmem_limit_bytes=VMEM_LIMIT),
        name="solve_near",
    )(*pieces, root)


def solve_scratch(size):
    return [
        pltpu.VMEM((size, size), f32),
        pltpu.VMEM((2 * BUF_ROWS, size), f32),
        pltpu.VMEM((size, size), f32),
        pltpu.VMEM((size, size), f32),
    ]


def solve_kernel(places, *refs):
    count = len(places)
    pieces = refs[:count]
    inverse, near, shift, target, root, weights = refs[count : count + 6]
    fwd, gram, buf, low, scaled, second, far_z, right, out = refs[count + 6 :]
    rows = pieces[0].shape[0]
    own, size = target.shape[0], near.shape[0]
    members = 2 * size
    own_core, own_side = own_bits()

    def start(place):
        far, dy, dc = place
        core = own_core if dc == 0 else 1 - own_core
        side = own_side if dy == 0 else 1 - own_side
        return pl.multiple_of(far * own + (core * 2 + side) * rows, SUB)

    for piece, place in zip(pieces, places):
        if place[0] == 0:
            fwd[pl.ds(start(place), rows), :] = piece[...]
    scale = root[0:1, :]
    for i, piece in enumerate(pieces[count // 2 :]):
        far_z[i * rows : (i + 1) * rows, :] = (piece[...] - shift[0:1, :]) * scale
    residual = (target[...] - fwd[...]) * scale
    za, zb = near[...], far_z[...]
    side = dot3(zb, za, ((1,), (1,)))
    ca, cb = dot3(za, residual, ((1,), (1,))), dot3(zb, residual, ((1,), (1,)))
    mean = (jnp.sum(ca, axis=0, keepdims=True) + jnp.sum(cb, axis=0, keepdims=True)) / members
    ones = jnp.ones((size, own), f32)
    ra = jnp.concatenate([ca - mean, ones], axis=1)
    rb = jnp.concatenate([cb - mean, ones], axis=1)
    top = dot3(inverse[...], jnp.concatenate([side.T, ra], axis=1), ((1,), (0,)))
    drop = dot3(side, top, ((1,), (0,)))
    gram[...] = add_diagonal(dot3(zb, zb, ((1,), (1,))), float(members - 1)) - drop[:, :size]
    right[0:size, :] = top
    right[size:, size:] = rb - drop[:, size:]
    set_inverse(second, gram, buf, low, scaled)
    xb = dot3(second[...], right[size:, size:], ((1,), (0,)))
    xa = right[0:size, size:] - dot3(right[0:size, 0:size], xb, ((1,), (0,)))
    x = jnp.concatenate([xa, xb], axis=0)
    w, unit = x[:, :own], x[:, own:]
    w = w - unit * (jnp.sum(w, axis=0, keepdims=True) / jnp.sum(unit, axis=0, keepdims=True))
    w = w - jnp.mean(w, axis=0, keepdims=True)
    for i, place in enumerate(places):
        out[pl.ds(start(place), rows), :] = w[i * rows : (i + 1) * rows, :]
    weights[...] = out[...].T


def solve(pieces, places, inverse, near, shift, target, root):
    own, cols = target.shape
    size = near.shape[0]
    return pl.pallas_call(
        functools.partial(solve_kernel, places),
        out_shape=jax.ShapeDtypeStruct((own, 2 * size), f32),
        in_specs=[VMEM] * (len(pieces) + 5),
        out_specs=VMEM,
        scratch_shapes=[pltpu.VMEM((own, cols), f32)]
        + solve_scratch(size)
        + [
            pltpu.VMEM((size, size), f32),
            pltpu.VMEM((size, cols), f32),
            pltpu.VMEM((2 * size, size + 2 * own), f32),
            pltpu.VMEM((2 * size, own), f32),
        ],
        cost_estimate=pl.CostEstimate(flops=5_000_000_000, bytes_accessed=1, transcendentals=0),
        compiler_params=pltpu.CompilerParams(vmem_limit_bytes=VMEM_LIMIT),
        name="solve",
    )(*pieces, inverse, near, shift, target, root)


def update_kernel(weights, own_ens, *refs):
    parts = len(CUTS) - 1
    others, (out, buf, sems) = refs[:-3], refs[-3:]
    width = out.shape[1] // PARTS
    w_high, w_low = halves(weights[...])
    copies = []
    for part in range(parts):
        first, end = CUTS[part : part + 2]
        for i in range(first, end, STEP):
            last = min(i + STEP, end)
            cols = slice(i * width, last * width)
            at = slice((i - first) * width, (last - first) * width)
            held = [own_ens[:, cols]] + [ref[:, at] for ref in others[part::parts]]
            high, low = halves(jnp.concatenate(held, axis=0))
            change = matmul(w_high, high) + (matmul(w_high, low) + matmul(w_low, high))
            buf[:, cols] = held[0] + change
            copies.append(pltpu.make_async_copy(buf.at[:, cols], out.at[:, cols], sems.at[i]))
            copies[-1].start()
    for copy in copies:
        copy.wait()


def update(weights, own_ens, others):
    own, params = own_ens.shape
    return pl.pallas_call(
        update_kernel,
        out_shape=jax.ShapeDtypeStruct((own, params), f32),
        in_specs=[VMEM] * (2 + len(others)),
        out_specs=HBM,
        scratch_shapes=[pltpu.VMEM((own, params), f32), pltpu.SemaphoreType.DMA((PARTS,))],
        cost_estimate=pl.CostEstimate(
            flops=2 * own * weights.shape[1] * params, bytes_accessed=4 * params * (own + weights.shape[1]), transcendentals=0
        ),
        compiler_params=pltpu.CompilerParams(vmem_limit_bytes=VMEM_LIMIT),
        name="update",
    )(weights, own_ens, *others)


def per_device(n_mem, n_par, operator, ensemble, noise, observations, variances, rows):
    index = lax.axis_index("par")
    side = lax.bitwise_and(lax.shift_right_logical(index, 1), 1)

    def swap(x, far, near):
        pairs = [
            (m * n_par + p, (m ^ far) * n_par + (p ^ near)) for m in range(n_mem) for p in range(n_par)
        ]
        return lax.ppermute(x, ("mem", "par"), pairs)

    width = ensemble.shape[1] // PARTS
    first, second, third, last = (ensemble[:, width * i : width * k] for i, k in zip(CUTS, CUTS[1:]))
    first = [swap(first, far, 0) for far in range(1, n_mem)]
    second = [swap(second, far, 0) for far in range(1, n_mem)]
    keep, send = forward(ensemble, operator)
    part = keep + swap(send, 0, 1)
    size = part.shape[0] // 2
    other = swap(lax.dynamic_slice_in_dim(part, (1 - side) * size, size, 0), 0, 2)
    other, first = lax.optimization_barrier((other, first))
    total = lax.dynamic_slice_in_dim(part, side * size, size, 0) + other
    target, root = lookup(rows, observations, variances, noise)
    stride = 4
    while stride < n_par:
        ways = min(4, n_par // stride)
        terms = [total] + [swap(total, 0, d * stride) for d in range(1, ways)]
        if stride == 4:
            third, total = lax.optimization_barrier((third, total))
            third = [swap(third, far, 0) for far in range(1, n_mem)]
            terms, target, root, second = lax.optimization_barrier((terms, target, root, second))
        total = add_all(terms)
        stride *= ways
    places = [(far, dy, 0) for far in range(n_mem) for dy in range(2)]
    pieces = [total if (far, dy) == (0, 0) else swap(total, far, 2 * dy) for far, dy, _ in places]
    last, _ = lax.optimization_barrier((last, total))
    last = [swap(last, far, 0) for far in range(1, n_mem)]
    inverse, near, shift = solve_near(pieces, root, ensemble.shape[0] * n_mem)
    mine, pieces[1], third = lax.optimization_barrier((pieces[0], pieces[1], third))
    pieces += [swap(piece, 0, 1) for piece in [mine] + pieces[1:]]
    places += [(far, dy, 1) for far, dy, _ in places]
    weights = solve(pieces, places, inverse, near, shift, target, root)
    return update(weights, ensemble, [part for far in zip(first, second, third, last) for part in far])


def solution(mesh):
    return jax.shard_map(
        functools.partial(per_device, mesh.shape["mem"], mesh.shape["par"]),
        mesh=mesh,
        in_specs=(P("par", None), P("mem", "par"), P("mem", None), P(), P(), P()),
        out_specs=P("mem", "par"),
        check_vma=False,
    )
```

```python
import functools

import jax
import jax.numpy as jnp
from jax import lax
from jax.experimental import pallas as pl
from jax.experimental.pallas import tpu as pltpu
from jax.sharding import PartitionSpec as P

f32 = jnp.float32
HIGHEST = lax.Precision.HIGHEST
SUB, LANE = 8, 128
BUF_ROWS = 2 * SUB * SUB + SUB
FAR_ROWS = 4
VMEM = pl.BlockSpec(memory_space=pltpu.VMEM)
HBM = pl.BlockSpec(memory_space=pltpu.HBM)
VMEM_LIMIT = 20 << 20
PARTS = 16
CUTS = (0, 1, 6, 9, 16)
STEP = 4


def dot(a, b, dims, precision=HIGHEST):
    return lax.dot_general(a, b, (dims, ((), ())), precision=precision, preferred_element_type=f32)


def add_all(terms):
    terms = list(terms)
    while len(terms) > 1:
        pairs = [terms[i] + terms[i + 1] for i in range(0, len(terms) - 1, 2)]
        terms = pairs + ([terms[-1]] if len(terms) % 2 else [])
    return terms[0]


def pivot_rows(e, sets):
    n = len(e)
    e = [list(line) for line in e]
    sets = [list(rows) for rows in sets]
    low = [[None] * n for _ in range(n)]
    outs = [[None] * n for _ in sets]
    for a in range(0, n, 2):
        b = a + 1
        scale = 1.0 / (e[a][a] * e[b][b] - e[a][b] * e[a][b])
        aa, bb, ab = e[b][b] * scale, e[a][a] * scale, -(e[a][b] * scale)
        for rows, out in zip(sets, outs):
            out[a] = aa * rows[a] + ab * rows[b]
            out[b] = ab * rows[a] + bb * rows[b]
        for i in range(b + 1, n):
            la = e[a][i] * aa + e[b][i] * ab
            lb = e[a][i] * ab + e[b][i] * bb
            low[i][a], low[i][b] = la, lb
            for m in range(i, n):
                e[i][m] = e[i][m] - (la * e[a][m] + lb * e[b][m])
            for rows in sets:
                rows[i] = rows[i] - (la * rows[a] + lb * rows[b])
    for a in range(n - 4, -1, -2):
        for k in (a, a + 1):
            for out in outs:
                out[k] = out[k] - add_all(low[i][k] * out[i] for i in range(a + 2, n))
    return outs


def across(v, k):
    return jnp.broadcast_to(v[:, k : k + 1], v.shape)


def block_inverse(matrix, buf):
    size = matrix.shape[0]
    lane = lax.broadcasted_iota(jnp.int32, (SUB, size), 1)
    sub = lax.broadcasted_iota(jnp.int32, (SUB, size), 0)
    n = size // SUB
    square = SUB * SUB
    m = [matrix[SUB * i : SUB * (i + 1), :] for i in range(n)]
    low, scaled = [], []
    cols = [across(m[0], k) for k in range(SUB)]
    for j in range(n):
        at = SUB * j
        here = (lane >= at) & (lane < at + SUB)
        base = (j % 2) * BUF_ROWS

        def put(start, values):
            for k, value in enumerate(values):
                buf[base + start + SUB * k : base + start + SUB * (k + 1), :] = value

        def get(i):
            return jnp.broadcast_to(buf[base + i : base + i + 1, :], (SUB, size))

        put(0, cols)
        row = jnp.where(here, (lane - at == sub).astype(f32), m[j])
        put(2 * square, [row])
        e = [[get(SUB * k + i) if i <= k else None for k in range(SUB)] for i in range(SUB)]
        sets = [[get(2 * square + k) for k in range(SUB)]]
        if j + 1 < n:
            side = [across(m[j + 1], at + k) for k in range(SUB)]
            old = [across(m[j + 1], at + SUB + k) for k in range(SUB)]
            put(square, side)
            sets.append(side)
        outs = pivot_rows(e, sets)
        new = outs[0]
        if j + 1 < n:
            cols = [
                old[i] - add_all(get(square + SUB * k + i) * outs[1][k] for k in range(SUB)) for i in range(SUB)
            ]
            m[j + 1] = jnp.where(here, 0.0, m[j + 1]) - add_all(side[k] * new[k] for k in range(SUB))
        done = new[0]
        for i in range(1, SUB):
            done = jnp.where(sub == i, new[i], done)
        far = j + 3 if n - j - 3 >= FAR_ROWS else n
        for i in range(j + 2, min(far, n)):
            m[i] = jnp.where(here, 0.0, m[i]) - add_all(across(m[i], at + k) * new[k] for k in range(SUB))
        if far < n:
            blank = lambda count: [jnp.zeros((count, size), f32)] if count else []
            rows = jnp.concatenate(blank(at) + [done] + blank(size - at - SUB), axis=0)
            drop = dot3(jnp.concatenate(m[far:], axis=0), rows, ((1,), (0,)))
            for i in range(far, n):
                m[i] = jnp.where(here, 0.0, m[i]) - drop[SUB * (i - far) : SUB * (i - far + 1), :]
        keep = lane < at + SUB
        low.append(jnp.where(keep, row, 0.0))
        scaled.append(jnp.where(keep, done, 0.0))
    return jnp.concatenate(low, axis=0), jnp.concatenate(scaled, axis=0)


def own_bits():
    index = lax.axis_index("par")
    return lax.bitwise_and(index, 1), lax.bitwise_and(lax.shift_right_logical(index, 1), 1)


def halves(x):
    high = x.astype(jnp.bfloat16)
    return high, (x - high.astype(f32)).astype(jnp.bfloat16)


def matmul(a, b, dims=((1,), (0,))):
    return lax.dot_general(a, b, (dims, ((), ())), preferred_element_type=f32)


def dot3(a, b, dims):
    (ah, al), (bh, bl) = halves(a), halves(b)
    return matmul(ah, bh, dims) + (matmul(ah, bl, dims) + matmul(al, bh, dims))


def own_bits():
    index = lax.axis_index("par")
    return lax.bitwise_and(index, 1), lax.bitwise_and(lax.shift_right_logical(index, 1), 1)


def dot3(a, b, dims):
    parts = []
    for x in (a, b):
        high = x.astype(jnp.bfloat16)
        parts.append((high, (x - high.astype(f32)).astype(jnp.bfloat16)))
    (ah, al), (bh, bl) = parts
    mul = lambda x, y: lax.dot_general(x, y, (dims, ((), ())), preferred_element_type=f32)
    return mul(ah, bh) + (mul(ah, bl) + mul(al, bh))


def own_bits():
    index = lax.axis_index("par")
    return lax.bitwise_and(index, 1), lax.bitwise_and(lax.shift_right_logical(index, 1), 1)


def forward_kernel(steps, ens, op, keep, send, ens_buf, op_buf, acc, sems):
    depth = op.shape[0] // steps
    cut = lambda i: pl.ds(i * depth, depth)
    copies = [pltpu.make_async_copy(ens, ens_buf, sems.at[steps])]
    copies += [pltpu.make_async_copy(op.at[cut(i), :], op_buf.at[cut(i), :], sems.at[i]) for i in range(steps)]
    for copy in copies:
        copy.start()
    copies[0].wait()
    total = None
    for i in range(steps):
        copies[i + 1].wait()
        term = dot3(ens_buf[:, cut(i)], op_buf[cut(i), :], ((1,), (0,)))
        total = term if total is None else total + term
    acc[...] = total
    half = keep.shape[0]
    core, _ = own_bits()
    keep[...] = acc[pl.ds(pl.multiple_of(core * half, SUB), half), :]
    send[...] = acc[pl.ds(pl.multiple_of((1 - core) * half, SUB), half), :]


def forward(ens, op):
    members, params = ens.shape
    rows = op.shape[1]
    steps = 8 if params % (8 * LANE) == 0 else 1
    half = jax.ShapeDtypeStruct((members // 2, rows), f32)
    return pl.pallas_call(
        functools.partial(forward_kernel, steps),
        out_shape=(half, half),
        in_specs=[HBM, HBM],
        out_specs=(VMEM, VMEM),
        scratch_shapes=[
            pltpu.VMEM(ens.shape, f32),
            pltpu.VMEM(op.shape, f32),
            pltpu.VMEM((members, rows), f32),
            pltpu.SemaphoreType.DMA((steps + 1,)),
        ],
        cost_estimate=pl.CostEstimate(
            flops=2 * members * params * rows, bytes_accessed=4 * (members * params + params * rows), transcendentals=0
        ),
        compiler_params=pltpu.CompilerParams(vmem_limit_bytes=VMEM_LIMIT),
        name="forward",
    )(pltpu.with_memory_space_constraint(ens, pltpu.HBM), pltpu.with_memory_space_constraint(op, pltpu.HBM))


def lookup_kernel(rows, obs, var, noise, target, root):
    index = rows[...]
    high = lax.shift_right_logical(index, 7)
    low = lax.bitwise_and(index, LANE - 1)
    count = index.shape[1]
    blocks = obs.shape[0]
    pick_high = (lax.broadcasted_iota(jnp.int32, (blocks, count), 0) == high).astype(f32)
    pick_low = (lax.broadcasted_iota(jnp.int32, (LANE, count), 0) == low).astype(f32)
    obs_rows = jnp.sum(dot(obs[...], pick_high, ((0,), (0,))) * pick_low, axis=0, keepdims=True)
    var_rows = jnp.sum(dot(var[...], pick_high, ((0,), (0,))) * pick_low, axis=0, keepdims=True)
    target[...] = obs_rows + jnp.sqrt(var_rows) * noise[...]
    root[...] = jnp.broadcast_to(lax.rsqrt(var_rows), root.shape)


def lookup(rows, obs, var, noise):
    count = rows.shape[0]
    return pl.pallas_call(
        lookup_kernel,
        out_shape=(
            jax.ShapeDtypeStruct(noise.shape, f32),
            jax.ShapeDtypeStruct((SUB, count), f32),
        ),
        in_specs=[VMEM] * 4,
        out_specs=(VMEM, VMEM),
        cost_estimate=pl.CostEstimate(flops=2 * obs.shape[0] * LANE * count * 12, bytes_accessed=1 << 20, transcendentals=0),
        compiler_params=pltpu.CompilerParams(vmem_limit_bytes=VMEM_LIMIT),
        name="lookup",
    )(rows.reshape(1, count), obs.reshape(-1, LANE), var.reshape(-1, LANE), noise)


def fenced(body):
    pl.when(lax.axis_index("par") >= 0)(body)


def set_inverse(out, matrix, buf, low, scaled):
    @fenced
    def _():
        low[...], scaled[...] = block_inverse(matrix[...], buf)

    out[...] = dot3(low[...], scaled[...], ((0,), (0,)))


def add_diagonal(matrix, value):
    row = lax.broadcasted_iota(jnp.int32, matrix.shape, 0)
    col = lax.broadcasted_iota(jnp.int32, matrix.shape, 1)
    return matrix + jnp.where(row == col, value, 0.0)


def near_kernel(members, count, *refs):
    pieces = refs[:count]
    root, inverse, near, shift, gram, buf, low, scaled = refs[count:]
    rows = pieces[0].shape[0]
    for i, piece in enumerate(pieces):
        near[i * rows : (i + 1) * rows, :] = piece[...]
    mean = jnp.mean(near[...], axis=0, keepdims=True)
    shift[...] = jnp.broadcast_to(mean, shift.shape)
    z = (near[...] - mean) * root[0:1, :]
    near[...] = z
    gram[...] = add_diagonal(dot3(z, z, ((1,), (1,))), float(members - 1))
    set_inverse(inverse, gram, buf, low, scaled)


def solve_near(pieces, root, members):
    rows, cols = pieces[0].shape
    size = rows * len(pieces)
    square = jax.ShapeDtypeStruct((size, size), f32)
    return pl.pallas_call(
        functools.partial(near_kernel, members, len(pieces)),
        out_shape=(square, jax.ShapeDtypeStruct((size, cols), f32), jax.ShapeDtypeStruct((SUB, cols), f32)),
        in_specs=[VMEM] * (len(pieces) + 1),
        out_specs=(VMEM, VMEM, VMEM),
        scratch_shapes=solve_scratch(size),
        cost_estimate=pl.CostEstimate(flops=5_000_000_000, bytes_accessed=1, transcendentals=0),
        compiler_params=pltpu.CompilerParams(vmem_limit_bytes=VMEM_LIMIT),
        name="solve_near",
    )(*pieces, root)


def solve_scratch(size):
    return [
        pltpu.VMEM((size, size), f32),
        pltpu.VMEM((2 * BUF_ROWS, size), f32),
        pltpu.VMEM((size, size), f32),
        pltpu.VMEM((size, size), f32),
    ]


def solve_kernel(places, *refs):
    count = len(places) // 2
    pieces = list(refs[:count])
    far_rows, inverse, near, shift, target, root, weights = refs[count : count + 7]
    fwd, gram, buf, low, scaled, second, far_z, right, out = refs[count + 7 :]
    pieces += [far_rows.at[i * pieces[0].shape[0] : (i + 1) * pieces[0].shape[0], :] for i in range(count)]
    rows = pieces[0].shape[0]
    own, size = target.shape[0], near.shape[0]
    members = 2 * size
    own_core, own_side = own_bits()

    def start(place):
        far, dy, dc = place
        core = own_core if dc == 0 else 1 - own_core
        side = own_side if dy == 0 else 1 - own_side
        return pl.multiple_of(far * own + (core * 2 + side) * rows, SUB)

    for piece, place in zip(pieces, places):
        if place[0] == 0:
            fwd[pl.ds(start(place), rows), :] = piece[...]
    scale = root[0:1, :]
    far_z[...] = (far_rows[...] - shift[0:1, :]) * scale
    residual = (target[...] - fwd[...]) * scale
    za, zb = near[...], far_z[...]
    side = dot3(zb, za, ((1,), (1,)))
    ca, cb = dot3(za, residual, ((1,), (1,))), dot3(zb, residual, ((1,), (1,)))
    mean = (jnp.sum(ca, axis=0, keepdims=True) + jnp.sum(cb, axis=0, keepdims=True)) / members
    ones = jnp.ones((size, own), f32)
    ra = jnp.concatenate([ca - mean, ones], axis=1)
    rb = jnp.concatenate([cb - mean, ones], axis=1)
    top = dot3(inverse[...], jnp.concatenate([side.T, ra], axis=1), ((1,), (0,)))
    drop = dot3(side, top, ((1,), (0,)))
    gram[...] = add_diagonal(dot3(zb, zb, ((1,), (1,))), float(members - 1)) - drop[:, :size]
    right[0:size, :] = top
    right[size:, size:] = rb - drop[:, size:]
    set_inverse(second, gram, buf, low, scaled)
    xb = dot3(second[...], right[size:, size:], ((1,), (0,)))
    xa = right[0:size, size:] - dot3(right[0:size, 0:size], xb, ((1,), (0,)))
    x = jnp.concatenate([xa, xb], axis=0)
    w, unit = x[:, :own], x[:, own:]
    w = w - unit * (jnp.sum(w, axis=0, keepdims=True) / jnp.sum(unit, axis=0, keepdims=True))
    w = w - jnp.mean(w, axis=0, keepdims=True)
    for i, place in enumerate(places):
        out[pl.ds(start(place), rows), :] = w[i * rows : (i + 1) * rows, :]
    weights[...] = out[...].T


def solve(pieces, far_rows, places, inverse, near, shift, target, root):
    own, cols = target.shape
    size = near.shape[0]
    return pl.pallas_call(
        functools.partial(solve_kernel, places),
        out_shape=jax.ShapeDtypeStruct((own, 2 * size), f32),
        in_specs=[VMEM] * (len(pieces) + 6),
        out_specs=VMEM,
        scratch_shapes=[pltpu.VMEM((own, cols), f32)]
        + solve_scratch(size)
        + [
            pltpu.VMEM((size, size), f32),
            pltpu.VMEM((size, cols), f32),
            pltpu.VMEM((2 * size, size + 2 * own), f32),
            pltpu.VMEM((2 * size, own), f32),
        ],
        cost_estimate=pl.CostEstimate(flops=5_000_000_000, bytes_accessed=1, transcendentals=0),
        compiler_params=pltpu.CompilerParams(vmem_limit_bytes=VMEM_LIMIT),
        name="solve",
    )(*pieces, far_rows, inverse, near, shift, target, root)


def update_kernel(weights, own_ens, *refs):
    parts = len(CUTS) - 1
    others, (out, buf, sems) = refs[:-3], refs[-3:]
    width = out.shape[1] // PARTS
    w_high, w_low = halves(weights[...])
    copies = []
    for part in range(parts):
        first, end = CUTS[part : part + 2]
        for i in range(first, end, STEP):
            last = min(i + STEP, end)
            cols = slice(i * width, last * width)
            at = slice((i - first) * width, (last - first) * width)
            held = [own_ens[:, cols]] + [ref[:, at] for ref in others[part::parts]]
            high, low = halves(jnp.concatenate(held, axis=0))
            change = matmul(w_high, high) + (matmul(w_high, low) + matmul(w_low, high))
            buf[:, cols] = held[0] + change
            copies.append(pltpu.make_async_copy(buf.at[:, cols], out.at[:, cols], sems.at[i]))
            copies[-1].start()
    for copy in copies:
        copy.wait()


def update(weights, own_ens, others):
    own, params = own_ens.shape
    return pl.pallas_call(
        update_kernel,
        out_shape=jax.ShapeDtypeStruct((own, params), f32),
        in_specs=[VMEM] * (2 + len(others)),
        out_specs=HBM,
        scratch_shapes=[pltpu.VMEM((own, params), f32), pltpu.SemaphoreType.DMA((PARTS,))],
        cost_estimate=pl.CostEstimate(
            flops=2 * own * weights.shape[1] * params, bytes_accessed=4 * params * (own + weights.shape[1]), transcendentals=0
        ),
        compiler_params=pltpu.CompilerParams(vmem_limit_bytes=VMEM_LIMIT),
        name="update",
    )(weights, own_ens, *others)


def per_device(n_mem, n_par, operator, ensemble, noise, observations, variances, rows):
    index = lax.axis_index("par")
    side = lax.bitwise_and(lax.shift_right_logical(index, 1), 1)

    def swap(x, far, near):
        pairs = [
            (m * n_par + p, (m ^ far) * n_par + (p ^ near)) for m in range(n_mem) for p in range(n_par)
        ]
        return lax.ppermute(x, ("mem", "par"), pairs)

    width = ensemble.shape[1] // PARTS
    first, second, third, last = (ensemble[:, width * i : width * k] for i, k in zip(CUTS, CUTS[1:]))
    first = [swap(first, far, 0) for far in range(1, n_mem)]
    second = [swap(second, far, 0) for far in range(1, n_mem)]
    keep, send = forward(ensemble, operator)
    part = keep + swap(send, 0, 1)
    size = part.shape[0] // 2
    other = swap(lax.dynamic_slice_in_dim(part, (1 - side) * size, size, 0), 0, 2)
    other, first = lax.optimization_barrier((other, first))
    total = lax.dynamic_slice_in_dim(part, side * size, size, 0) + other
    target, root = lookup(rows, observations, variances, noise)
    stride = 4
    while stride < n_par:
        ways = min(4, n_par // stride)
        terms = [total] + [swap(total, 0, d * stride) for d in range(1, ways)]
        if stride == 4:
            third, total = lax.optimization_barrier((third, total))
            third = [swap(third, far, 0) for far in range(1, n_mem)]
            terms, target, root, second = lax.optimization_barrier((terms, target, root, second))
        total = add_all(terms)
        stride *= ways
    places = [(far, dy, 0) for far in range(n_mem) for dy in range(2)]
    pieces = [total if (far, dy) == (0, 0) else swap(total, far, 2 * dy) for far, dy, _ in places]
    last, _ = lax.optimization_barrier((last, total))
    last = [swap(last, far, 0) for far in range(1, n_mem)]
    inverse, near, shift = solve_near(pieces, root, ensemble.shape[0] * n_mem)
    third, pieces[1] = lax.optimization_barrier((third, pieces[1]))
    far_rows = swap(jnp.concatenate(pieces, axis=0), 0, 1)
    places += [(far, dy, 1) for far, dy, _ in places]
    weights = solve(pieces, far_rows, places, inverse, near, shift, target, root)
    return update(weights, ensemble, [part for far in zip(first, second, third, last) for part in far])


def solution(mesh):
    return jax.shard_map(
        functools.partial(per_device, mesh.shape["mem"], mesh.shape["par"]),
        mesh=mesh,
        in_specs=(P("par", None), P("mem", "par"), P("mem", None), P(), P(), P()),
        out_specs=P("mem", "par"),
        check_vma=False,
    )
```
